32 devices in a mesh: dp: 8 (over y, x, core), expert: 4 (over z).
Axes of the slice: x: 2, y: 2, z: 4, core: 2. Of those that a mesh axis runs over, the one named last changes fastest.
Arguments:
- tokens: bfloat16 [256, 4096], P(('dp', 'expert')), may hold values from -6 to 6
- expert_ids: int32 [256, 8], P(('dp', 'expert')), may hold values from 0 to 15, all different within a row; in each aligned block of 8 rows (0 to 7, 8 to 15, ...) at most 8 rows name the same one
- router: bfloat16 [16, 4096], replicated, may hold values from -0.09375 to 0.09375
- w_gate: bfloat16 [16, 1536, 4096], P('dp', 'expert'), may hold values from -0.09375 to 0.09375
- w_up: bfloat16 [16, 1536, 4096], P('dp', 'expert'), may hold values from -0.09375 to 0.09375
- w_down: bfloat16 [16, 1536, 4096], P('dp', 'expert'), may hold values from -0.15625 to 0.15625
Outputs:
- mixed: bfloat16 [256, 4096], P(('dp', 'expert'))
The draws below stay inside these ranges and needn't reach their ends.
Inputs may be any that keep to these rules, and one draw needn't show every extreme that they name: `expert_ids`: each row names 8 different experts. Within the rows of one device (aligned blocks of 8 rows) no expert is named by more than 8 rows, and in some block one expert is named by exactly 8 rows.
All inputs are finite; a program needn't handle non-finite values.
Results may differ from the reference program's by a relative error of at most 0.0049.
Values may be sent and summed in bfloat16 or wider, within the bound.
No kernel may reach another device: no remote copies, remote signals or barrier semaphores. Data moves between devices by JAX's collectives and lax.ppermute only.
A program may use at most 192 MiB of HBM per device.

```python
import math
import jax
import jax.numpy as jnp
import numpy as np
from jax import lax

D = 4096
FF = 1536
TOPK = 8
TOK_DEV = 8
TOKENS = 256
EXPERTS = 16
CAP = 8


def levels(rng, dims, cuts, least, top_value):
    gain, own = 1.0, jax.random.fold_in(rng, 6)
    for position, blocks in cuts:
        heights = jnp.exp(jax.random.uniform(jax.random.fold_in(own, position), (blocks,), jnp.float32, least / len(cuts), top_value / len(cuts)))
        gain = gain * jnp.repeat(heights, dims[position] // blocks).reshape([-1 if axis == position else 1 for axis in range(len(dims))])
    return gain


def deal_out(stream_key, own, number, rows, count, top, bound, lean):
    sequence = jax.random.permutation(stream_key, count)
    packed, ordinary = load_shares(count, rows * top, bound, lean, True), load_shares(count, rows * top, bound, lean, False)
    places = jnp.arange(count)

    def named(tallies, rotation):
        used = int((tallies > 0).sum())
        fixed = max(1, used // 4)
        moved = fixed + (places - fixed + rotation * (used - fixed)) % max(1, count - fixed)
        return jnp.zeros((count,), jnp.int32).at[sequence[jnp.where(places < fixed, places, moved)]].set(jnp.asarray(tallies, jnp.int32))

    tallies = jnp.where(number % 4 == 0, named(packed, number // 4), named(ordinary, number - number // 4 - 1))
    mixed = jax.random.permutation(jax.random.fold_in(own, 3), count)
    source_of, sink = mixed[0:count // 2 * 2:2], mixed[1:count // 2 * 2:2]
    room = jnp.minimum(tallies[source_of] - 1, bound - tallies[sink]) // 2
    room = jnp.where((source_of == sequence[0]) | (sink == sequence[0]) | (tallies[sink] == 0), 0, jnp.maximum(room, 0))
    moved = jax.random.randint(jax.random.fold_in(own, 4), (count // 2,), 0, 1 << 20) % (room + 1)
    tallies = tallies.at[source_of].add(-moved).at[sink].add(moved)
    items = jnp.searchsorted(jnp.cumsum(tallies), jnp.arange(rows * top), side="right").astype(jnp.int32)
    listing = items.reshape(top, rows).T
    listing = listing[jax.random.permutation(jax.random.fold_in(own, 1), rows)]
    rotation = jax.random.randint(jax.random.fold_in(own, 2), (rows, 1), 0, top)
    return jnp.take_along_axis(listing, (jnp.arange(top)[None, :] + rotation) % top, axis=1)


def load_shares(number_of, total, bound, slope, full):
    portions = [(1 << 20) // math.isqrt(grade ** slope) + 1 for grade in range(1, number_of + 1)]
    largest = bound if full else min(bound, max(-(-total // number_of), total * portions[0] // sum(portions)))
    least = 1 if total - largest >= number_of - 1 else 0
    holding, spare = [largest] + [least] * (number_of - 1), total - largest - least * (number_of - 1)
    while spare > 0:
        candidates = [i for i in range(1, number_of) if holding[i] < largest] or [i for i in range(1, number_of) if holding[i] < bound]
        pool, left = sum([portions[i] for i in candidates]), spare
        for i in candidates:
            addition = min(bound - holding[i], max(1, left * portions[i] // pool), spare)
            holding[i] = holding[i] + addition
            spare = spare - addition
    return np.array(holding)


def gaussian(key, extent, deviation, bound, pieces=(), kind=jnp.bfloat16):
    gain = levels(key, extent, pieces, -0.22, 0.18) if pieces else 1.0
    result = jax.random.normal(key, extent, jnp.float32) * deviation * gain
    return jnp.minimum(jnp.maximum(result, -bound), bound).astype(kind)


def setup_inputs(seed: int = 0) -> dict:
    seeds = jax.random.split(jax.random.key(seed), 7)
    tokens = gaussian(seeds[0], (TOKENS, D), 1.0, 6.0, ((0, 32),))
    expert_ids_keys = jax.random.split(jax.random.fold_in(seeds[1], 1), TOKENS // TOK_DEV)
    expert_ids_turns = jax.random.permutation(jax.random.fold_in(seeds[1], 3), TOKENS // TOK_DEV)
    expert_ids = jax.vmap(lambda own, number: deal_out(jax.random.fold_in(seeds[1], 2), own, number, TOK_DEV, EXPERTS, TOPK, CAP, 2))(expert_ids_keys, expert_ids_turns).reshape((TOKENS, TOPK))
    router = gaussian(seeds[2], (EXPERTS, D), D ** -0.5, 0.09375)
    w_gate = gaussian(seeds[3], (EXPERTS, FF, D), D ** -0.5, 0.09375, ((0, 8), (1, 4)))
    w_up = gaussian(seeds[4], (EXPERTS, FF, D), D ** -0.5, 0.09375, ((0, 8), (1, 4)))
    w_down = gaussian(seeds[5], (EXPERTS, FF, D), FF ** -0.5, 0.15625, ((0, 8), (1, 4)))
    return dict(tokens=tokens, expert_ids=expert_ids, router=router, w_gate=w_gate, w_up=w_up, w_down=w_down)


def times_rows(left, right):
    return lax.dot_general(left, right, (((1,), (1,)), ((), ())), preferred_element_type=jnp.float32)


def expert_ffn(picked_rows, gate_w, up_w, down_w):
    gate_proj = times_rows(picked_rows, gate_w)
    up_proj = times_rows(picked_rows, up_w)
    hidden = (jax.nn.silu(gate_proj) * up_proj).astype(jnp.bfloat16)
    return jnp.dot(hidden, down_w, preferred_element_type=jnp.float32)


def reference(tokens, expert_ids, router, w_gate, w_up, w_down):
    logits = times_rows(tokens, router)
    chosen = jnp.take_along_axis(logits, expert_ids, axis=1)
    scores = jax.nn.sigmoid(chosen)
    weight = scores / jnp.sum(scores, axis=1, keepdims=True)
    total_rows = tokens.shape[0]
    row_bound = (total_rows // TOK_DEV) * CAP

    def expert_step(summed_rows, expert):
        is_chosen = expert_ids == expert
        has_expert = jnp.any(is_chosen, axis=1)
        row_weight = jnp.sum(jnp.where(is_chosen, weight, 0.0), axis=1)
        row_index = jnp.nonzero(has_expert, size=row_bound, fill_value=total_rows)[0].astype(jnp.int32)
        picked_rows = jnp.take(tokens, row_index, axis=0, mode="fill", fill_value=0)
        expert_out = expert_ffn(picked_rows, w_gate[expert], w_up[expert], w_down[expert])
        scaled = expert_out * jnp.take(row_weight, row_index, mode="fill", fill_value=0)[:, None]
        return summed_rows.at[row_index].add(scaled, mode="drop"), None

    start = jnp.zeros((total_rows, tokens.shape[1]), jnp.float32)
    summed_rows, unused = lax.scan(expert_step, start, jnp.arange(EXPERTS, dtype=jnp.int32))
    return summed_rows.astype(jnp.bfloat16)
```

```python
import jax
import jax.numpy as jnp
from jax import lax
from jax.sharding import PartitionSpec as P

LANES = 128


def times_rows(left, right):
    return lax.dot_general(
        left, right, (((1,), (1,)), ((), ())), preferred_element_type=jnp.float32
    )


def swap(value, axis, bit):
    count = lax.axis_size(axis)
    return lax.ppermute(value, axis, [(i, i ^ (1 << bit)) for i in range(count)])


def axis_bits(axis):
    return list(range(lax.axis_size(axis).bit_length() - 1))


def routes():
    z_bits = [("expert", bit) for bit in reversed(axis_bits("expert"))]
    dp_bits = axis_bits("dp")
    core, plane = [("dp", bit) for bit in dp_bits[:1]], dp_bits[1:]
    x_bits = [("dp", bit) for bit in plane[: len(plane) // 2]]
    y_bits = [("dp", bit) for bit in plane[len(plane) // 2 :]]
    return z_bits, x_bits + y_bits, y_bits + x_bits, core[0]


def gather_rows(block):
    z_bits, first_way, second_way, core = routes()
    for step in z_bits[:-1]:
        block = jnp.concatenate([block, swap(block, *step)])
    first, second = block, swap(block, *z_bits[-1])
    for step_one, step_two in zip(first_way, second_way):
        other_first, other_second = swap(first, *step_one), swap(second, *step_two)
        first = jnp.concatenate([first, other_first])
        second = jnp.concatenate([second, other_second])
    return jnp.concatenate([first, second, swap(first, *core), swap(second, *core)])


def pass_on(part, step):
    half = part.shape[0] // 2
    return part[:half] + swap(part[half:].astype(jnp.bfloat16), *step).astype(jnp.float32)


def scatter_sums(total):
    z_bits, first_way, second_way, core = routes()
    half = total.shape[0] // 2
    quarter = half // 2
    away = total[half:].astype(jnp.bfloat16)
    first = total[:quarter] + swap(away[:quarter], *core).astype(jnp.float32)
    second = total[quarter:half] + swap(away[quarter:], *core).astype(jnp.float32)
    for step_one, step_two in zip(first_way[::-1], second_way[::-1]):
        first, second = pass_on(first, step_one), pass_on(second, step_two)
    part = jnp.concatenate([first, second])
    for step in z_bits[::-1]:
        part = pass_on(part, step)
    return part.astype(jnp.bfloat16)


def mixing_weights(tokens, ids, router):
    logits = times_rows(tokens, router)
    experts = lax.iota(jnp.int32, router.shape[0])
    chosen = jnp.any(ids[:, :, None] == experts[None, None, :], axis=1)
    scores = jnp.where(chosen, jax.nn.sigmoid(logits), 0.0)
    return scores / jnp.sum(scores, axis=1, keepdims=True)


def body(tokens, expert_ids, router, w_gate, w_up, w_down):
    exp_dev, _, width = w_gate.shape
    picks = expert_ids.shape[1]
    tags = jnp.pad(expert_ids.astype(jnp.bfloat16), ((0, 0), (0, LANES - picks)))
    packed = gather_rows(jnp.concatenate([tokens, tags], axis=1))
    rows, ids = packed[:, :width], packed[:, width : width + picks].astype(jnp.int32)
    mix = mixing_weights(rows, ids, router)
    mine = lax.dynamic_slice_in_dim(mix, lax.axis_index("dp") * exp_dev, exp_dev, axis=1)
    total = 0.0
    for local in range(exp_dev):
        gate = times_rows(rows, w_gate[local])
        up = times_rows(rows, w_up[local])
        hidden = (jax.nn.silu(gate) * up).astype(jnp.bfloat16)
        out = jnp.dot(hidden, w_down[local], preferred_element_type=jnp.float32)
        total = total + out * mine[:, local : local + 1]
    return scatter_sums(total)


def solution(mesh):
    in_specs = (
        P(("dp", "expert"), None),
        P(("dp", "expert"), None),
        P(),
        P("dp", "expert", None),
        P("dp", "expert", None),
        P("dp", "expert", None),
    )
    out_specs = P(("dp", "expert"), None)
    return jax.shard_map(body, mesh=mesh, in_specs=in_specs, out_specs=out_specs, check_vma=False)
```

```python
import functools

import jax
import jax.numpy as jnp
from jax import lax
from jax.experimental import pallas as pl
from jax.experimental.pallas import tpu as pltpu
from jax.sharding import PartitionSpec as P

LANES = 128
ROWS = 256
VMEM_BYTES = 32 * 1024 * 1024


def times_rows(left, right):
    return lax.dot_general(
        left, right, (((1,), (1,)), ((), ())), preferred_element_type=jnp.float32
    )


def swap(value, axis, bit):
    count = lax.axis_size(axis)
    return lax.ppermute(value, axis, [(i, i ^ (1 << bit)) for i in range(count)])


def axis_bits(axis):
    return list(range(lax.axis_size(axis).bit_length() - 1))


def routes():
    z_bits = [("expert", bit) for bit in reversed(axis_bits("expert"))]
    dp_bits = axis_bits("dp")
    core, plane = [("dp", bit) for bit in dp_bits[:1]], dp_bits[1:]
    x_bits = [("dp", bit) for bit in plane[: len(plane) // 2]]
    y_bits = [("dp", bit) for bit in plane[len(plane) // 2 :]]
    return z_bits, x_bits + y_bits, y_bits + x_bits, core[0]


def gather_rows(block, weights):
    z_bits, first_way, second_way, core = routes()
    weights = [hold(weight) for weight in weights]
    for index, step in enumerate(z_bits[:-1]):
        other = swap(block, *step)
        if index == 0:
            other, weights[0] = lax.optimization_barrier((other, weights[0]))
        block = jnp.concatenate([block, other])
    first, second = block, swap(block, *z_bits[-1])
    second, weights[1] = lax.optimization_barrier((second, weights[1]))
    for index, (step_one, step_two) in enumerate(zip(first_way, second_way)):
        other_first, other_second = swap(first, *step_one), swap(second, *step_two)
        if index == len(first_way) - 1:
            other_second, weights[2] = lax.optimization_barrier((other_second, weights[2]))
        first = jnp.concatenate([first, other_first])
        second = jnp.concatenate([second, other_second])
    return [first, second], [swap(first, *core), swap(second, *core)], weights


def pass_on(part, step):
    half = part.shape[0] // 2
    return part[:half] + swap(part[half:].astype(jnp.bfloat16), *step).astype(jnp.float32)


def scatter_sums(kept, away):
    z_bits, first_way, second_way, core = routes()
    first, second = [
        mine + swap(other, *core).astype(jnp.float32) for mine, other in zip(kept, away)
    ]
    for step_one, step_two in zip(first_way[::-1], second_way[::-1]):
        first, second = pass_on(first, step_one), pass_on(second, step_two)
    part = jnp.concatenate([first, second])
    for step in z_bits[::-1]:
        part = pass_on(part, step)
    return part.astype(jnp.bfloat16)


def expert_kernel(exp_dev, picks, parts, *refs):
    pieces, refs = refs[:parts], refs[parts:]
    router_ref, gate_ref, up_ref, down_ref = refs[:4]
    results, rows_ref = refs[4 : 4 + parts], refs[4 + parts]
    width = down_ref.shape[2]
    step = pieces[0].shape[0]
    for index, piece in enumerate(pieces):
        rows_ref[index * step : (index + 1) * step] = piece[...]
    rows = rows_ref[:, :width]
    ids = rows_ref[:, width:].astype(jnp.float32)
    logits = times_rows(rows, router_ref[...])
    experts = lax.broadcasted_iota(jnp.int32, logits.shape, 1)
    chosen = experts < 0
    for pick in range(picks):
        chosen = jnp.logical_or(chosen, ids[:, pick : pick + 1] == experts.astype(jnp.float32))
    scores = jnp.where(chosen, 1.0 / (1.0 + jnp.exp(-logits)), 0.0)
    mix = scores / jnp.sum(scores, axis=1, keepdims=True)
    first_expert = lax.axis_index("dp") * exp_dev
    hidden, shares = [], []
    for local in range(exp_dev):
        gate = times_rows(gate_ref[local], rows)
        up = times_rows(up_ref[local], rows)
        gated = gate / (1.0 + jnp.exp(-gate)) * up
        hidden.append(gated.T.astype(jnp.bfloat16))
        mine = jnp.where(experts == first_expert + local, mix, 0.0)
        shares.append(jnp.sum(mine, axis=1, keepdims=True))
    block = min(512, width)

    @pl.loop(0, width // block)
    def _(index):
        columns = pl.ds(pl.multiple_of(index * block, block), block)
        total = 0.0
        for local in range(exp_dev):
            out = jnp.dot(
                hidden[local], down_ref[local, :, columns], preferred_element_type=jnp.float32
            )
            total = total + out * shares[local]
        for part, result in enumerate(results):
            result[:, columns] = total[part * step : (part + 1) * step].astype(result.dtype)


def load_kernel(source_ref, held_ref, done):
    copy = pltpu.make_async_copy(source_ref, held_ref, done)
    copy.start()
    copy.wait()


def hold(weight):
    return pl.pallas_call(
        load_kernel,
        out_shape=pltpu.VMEM(weight.shape, weight.dtype),
        in_specs=[pl.BlockSpec(memory_space=pl.ANY)],
        out_specs=pl.BlockSpec(memory_space=pltpu.VMEM),
        scratch_shapes=[pltpu.SemaphoreType.DMA],
        compiler_params=pltpu.CompilerParams(vmem_limit_bytes=1024 * 1024),
        cost_estimate=pl.CostEstimate(
            flops=0, bytes_accessed=2 * weight.size * weight.dtype.itemsize, transcendentals=0
        ),
    )(pltpu.with_memory_space_constraint(weight, pltpu.HBM))


def run_experts(pieces, kinds, picks, router, w_gate, w_up, w_down):
    exp_dev, hidden_units, width = w_gate.shape
    rows = sum(piece.shape[0] for piece in pieces)
    in_vmem = pl.BlockSpec(memory_space=pltpu.VMEM)
    weights = [pltpu.with_memory_space_constraint(w, pltpu.VMEM) for w in (w_gate, w_up, w_down)]
    return pl.pallas_call(
        functools.partial(expert_kernel, exp_dev, picks, len(pieces)),
        out_shape=[
            jax.ShapeDtypeStruct((piece.shape[0], width), kind)
            for piece, kind in zip(pieces, kinds)
        ],
        in_specs=[in_vmem] * (len(pieces) + 4),
        out_specs=[in_vmem] * len(pieces),
        scratch_shapes=[pltpu.VMEM((rows, pieces[0].shape[1]), jnp.bfloat16)],
        compiler_params=pltpu.CompilerParams(vmem_limit_bytes=VMEM_BYTES),
        cost_estimate=pl.CostEstimate(
            flops=6 * rows * exp_dev * hidden_units * width,
            bytes_accessed=rows * width * 5,
            transcendentals=rows * exp_dev * hidden_units,
        ),
    )(*pieces, router, *weights)


def body(tokens, expert_ids, router, w_gate, w_up, w_down):
    picks = expert_ids.shape[1]
    tags = jnp.pad(expert_ids.astype(jnp.bfloat16), ((0, 0), (0, LANES - picks)))
    here, there, weights = gather_rows(
        jnp.concatenate([tokens, tags], axis=1), [w_gate, w_up, w_down]
    )
    pieces = here + there
    kinds = [jnp.float32] * len(here) + [jnp.bfloat16] * len(there)
    operands = (picks, router, *weights)
    if 4 * pieces[0].shape[0] <= ROWS:
        results = run_experts(pieces, kinds, *operands)
    else:
        results = []
        for piece, kind in zip(pieces, kinds):
            chunks = [
                run_experts([piece[start : start + ROWS]], [kind], *operands)[0]
                for start in range(0, piece.shape[0], ROWS)
            ]
            results.append(jnp.concatenate(chunks))
    return scatter_sums(results[: len(here)], results[len(here) :])


def solution(mesh):
    in_specs = (
        P(("dp", "expert"), None),
        P(("dp", "expert"), None),
        P(),
        P("dp", "expert", None),
        P("dp", "expert", None),
        P("dp", "expert", None),
    )
    out_specs = P(("dp", "expert"), None)
    return jax.shard_map(body, mesh=mesh, in_specs=in_specs, out_specs=out_specs, check_vma=False)
```

```python
import functools

import jax
import jax.numpy as jnp
from jax import lax
from jax.experimental import pallas as pl
from jax.experimental.pallas import tpu as pltpu
from jax.sharding import PartitionSpec as P

LANES = 128
ROWS = 256
COPIES = 4
VMEM_BYTES = 36 * 1024 * 1024
IN_VMEM = pl.BlockSpec(memory_space=pltpu.VMEM)
ANYWHERE = pl.BlockSpec(memory_space=pl.ANY)


def times_rows(left, right):
    return lax.dot_general(
        left, right, (((1,), (1,)), ((), ())), preferred_element_type=jnp.float32
    )


def swap(value, axis, mask):
    count = lax.axis_size(axis)
    return lax.ppermute(value, axis, [(i, i ^ mask) for i in range(count)])


def swap_sum(value, axis, mask):
    return swap(value.astype(jnp.bfloat16), axis, mask).astype(jnp.float32)


def squares():
    plane = [1 << bit for bit in range(1, lax.axis_size("dp").bit_length() - 1)]
    x_masks, y_masks = plane[: len(plane) // 2], plane[len(plane) // 2 :]
    return [(("dp", x), ("dp", y)) for x, y in zip(x_masks, y_masks)]


CORE = ("dp", 1)


def cat(parts):
    return parts[0] if len(parts) == 1 else jnp.concatenate(parts)


def split(value, count):
    step = value.shape[0] // count
    return [value[start : start + step] for start in range(0, value.shape[0], step)]


def gather_rows(block, w_gate, w_up):
    depth = lax.axis_size("expert")
    column = [block] + [swap(block, "expert", mask) for mask in range(1, depth)]
    near, far = cat(column[: depth // 2]), cat(column[depth // 2 :])
    near, held_gate = lax.optimization_barrier((near, hold(w_gate)))
    far, w_up = lax.optimization_barrier((far, w_up))
    held_up = hold(w_up)
    levels = squares()
    for level, (x, y) in enumerate(levels):
        near_x, near_y = swap(near, *x), swap(near, *y)
        far_x, far_y = swap(far, *x), swap(far, *y)
        if level == 0:
            near_x, far_y, held_up = lax.optimization_barrier((near_x, far_y, held_up))
        near_d, far_d = swap(near_x, *y), swap(far_y, *x)
        if level < len(levels) - 1:
            near, far = cat([near, near_x, near_y, near_d]), cat([far, far_x, far_y, far_d])
    groups = [cat([near, far]), cat([near_x, near_y, far_x, far_y]), cat([near_d, far_d])]
    return groups, [swap(group, *CORE) for group in groups], held_gate, held_up


def scatter_sums(kept, away):
    def joined(index):
        return kept[index] + swap(away[index], *CORE).astype(jnp.float32)

    near_d, far_d = split(joined(2), 2)
    near_x, near_y, far_x, far_y = split(joined(1), 4)
    near, far = split(joined(0), 2)
    levels = squares()[::-1]
    for level, (x, y) in enumerate(levels):
        if level > 0:
            near, near_x, near_y, near_d = split(near, 4)
            far, far_x, far_y, far_d = split(far, 4)
        far_y = far_y + swap_sum(far_d, *x)
        near_x = near_x + swap_sum(near_d, *y)
        far = far + swap_sum(far_x, *x) + swap_sum(far_y, *y)
        near = near + swap_sum(near_y, *y) + swap_sum(near_x, *x)
    depth = lax.axis_size("expert")
    total, *column = split(near, depth // 2) + split(far, depth // 2)
    for mask in range(depth - 1, 0, -1):
        total = total + swap_sum(column[mask - 1], "expert", mask)
    return total.astype(jnp.bfloat16)


def load_kernel(source_ref, held_ref, done):
    step = source_ref.shape[1] // COPIES
    copies = [
        pltpu.make_async_copy(
            source_ref.at[expert, pl.ds(part * step, step)],
            held_ref.at[expert, pl.ds(part * step, step)],
            done.at[expert * COPIES + part],
        )
        for expert in range(source_ref.shape[0])
        for part in range(COPIES)
    ]
    for copy in copies:
        copy.start()
    for copy in copies:
        copy.wait()


def hold(weight):
    return pl.pallas_call(
        load_kernel,
        out_shape=pltpu.VMEM(weight.shape, weight.dtype),
        in_specs=[ANYWHERE],
        out_specs=IN_VMEM,
        scratch_shapes=[pltpu.SemaphoreType.DMA((weight.shape[0] * COPIES,))],
        compiler_params=pltpu.CompilerParams(vmem_limit_bytes=1024 * 1024),
        cost_estimate=pl.CostEstimate(
            flops=0, bytes_accessed=2 * weight.size * weight.dtype.itemsize, transcendentals=0
        ),
    )(pltpu.with_memory_space_constraint(weight, pltpu.HBM))


def expert_kernel(exp_dev, picks, parts, *refs):
    pieces, refs = refs[:parts], refs[parts:]
    router_ref, gate_ref, up_ref, down_hbm = refs[:4]
    results, (rows_ref, down_ref, down_done) = refs[4 : 4 + parts], refs[4 + parts :]
    loads = [
        pltpu.make_async_copy(down_hbm.at[local], down_ref.at[local], down_done.at[local])
        for local in range(exp_dev)
    ]
    for load in loads:
        load.start()
    width = down_ref.shape[2]
    spans, start = [], 0
    for piece in pieces:
        spans.append((start, start + piece.shape[0]))
        rows_ref[start : start + piece.shape[0]] = piece[...]
        start += piece.shape[0]
    rows = rows_ref[:, :width]
    ids = rows_ref[:, width:].astype(jnp.float32)
    logits = times_rows(rows, router_ref[...])
    experts = lax.broadcasted_iota(jnp.int32, logits.shape, 1)
    chosen = experts < 0
    for pick in range(picks):
        chosen = jnp.logical_or(chosen, ids[:, pick : pick + 1] == experts.astype(jnp.float32))
    scores = jnp.where(chosen, 1.0 / (1.0 + jnp.exp(-logits)), 0.0)
    mix = scores / jnp.sum(scores, axis=1, keepdims=True)
    first_expert = lax.axis_index("dp") * exp_dev
    hidden, shares = [], []
    for local in range(exp_dev):
        gate = times_rows(gate_ref[local], rows)
        up = times_rows(up_ref[local], rows)
        gated = gate / (1.0 + jnp.exp(-gate)) * up
        hidden.append(gated.T.astype(jnp.bfloat16))
        mine = jnp.where(experts == first_expert + local, mix, 0.0)
        shares.append(jnp.sum(mine, axis=1, keepdims=True))
    for load in loads:
        load.wait()
    block = min(512, width)

    @pl.loop(0, width // block)
    def _(index):
        columns = pl.ds(pl.multiple_of(index * block, block), block)
        total = 0.0
        for local in range(exp_dev):
            out = jnp.dot(
                hidden[local], down_ref[local, :, columns], preferred_element_type=jnp.float32
            )
            total = total + out * shares[local]
        for (start, stop), result in zip(spans, results):
            result[:, columns] = total[start:stop].astype(result.dtype)


def run_experts(pieces, kinds, picks, router, held_gate, held_up, w_down):
    exp_dev, hidden_units, width = w_down.shape
    rows = sum(piece.shape[0] for piece in pieces)
    held = [pltpu.with_memory_space_constraint(w, pltpu.VMEM) for w in (held_gate, held_up)]
    down = pltpu.with_memory_space_constraint(w_down, pltpu.HBM)
    small = rows <= ROWS // 2 or len(pieces) > 1
    return pl.pallas_call(
        functools.partial(expert_kernel, exp_dev, picks, len(pieces)),
        out_shape=[
            (pltpu.VMEM if small else jax.ShapeDtypeStruct)((piece.shape[0], width), kind)
            for piece, kind in zip(pieces, kinds)
        ],
        in_specs=[IN_VMEM] * (len(pieces) + 3) + [ANYWHERE],
        out_specs=[IN_VMEM] * len(pieces),
        scratch_shapes=[
            pltpu.VMEM((rows, pieces[0].shape[1]), jnp.bfloat16),
            pltpu.VMEM(w_down.shape, w_down.dtype),
            pltpu.SemaphoreType.DMA((exp_dev,)),
        ],
        compiler_params=pltpu.CompilerParams(vmem_limit_bytes=VMEM_BYTES),
        cost_estimate=pl.CostEstimate(
            flops=6 * rows * exp_dev * hidden_units * width,
            bytes_accessed=rows * width * 5,
            transcendentals=rows * exp_dev * hidden_units,
        ),
    )(*pieces, router, *held, down)


def body(tokens, expert_ids, router, w_gate, w_up, w_down):
    picks = expert_ids.shape[1]
    tags = jnp.pad(expert_ids.astype(jnp.bfloat16), ((0, 0), (0, LANES - picks)))
    here, there, held_gate, held_up = gather_rows(
        jnp.concatenate([tokens, tags], axis=1), w_gate, w_up
    )
    pieces = here + there
    kinds = [jnp.float32] * len(here) + [jnp.bfloat16] * len(there)
    operands = (picks, router, held_gate, held_up, w_down)
    if sum(piece.shape[0] for piece in pieces) <= ROWS:
        results = run_experts(pieces, kinds, *operands)
    else:
        results = []
        for piece, kind in zip(pieces, kinds):
            chunks = [
                run_experts([piece[start : start + ROWS]], [kind], *operands)[0]
                for start in range(0, piece.shape[0], ROWS)
            ]
            results.append(cat(chunks))
    return scatter_sums(results[: len(here)], results[len(here) :])


def solution(mesh):
    in_specs = (
        P(("dp", "expert"), None),
        P(("dp", "expert"), None),
        P(),
        P("dp", "expert", None),
        P("dp", "expert", None),
        P("dp", "expert", None),
    )
    out_specs = P(("dp", "expert"), None)
    return jax.shard_map(body, mesh=mesh, in_specs=in_specs, out_specs=out_specs, check_vma=False)
```

```python
import functools

import jax
import jax.numpy as jnp
from jax import lax
from jax.experimental import pallas as pl
from jax.experimental.pallas import tpu as pltpu
from jax.sharding import PartitionSpec as P

LANES = 128
ROWS = 256
COPIES = 4
TERMS = 3
VMEM_BYTES = 36 * 1024 * 1024
IN_VMEM = pl.BlockSpec(memory_space=pltpu.VMEM)
ANYWHERE = pl.BlockSpec(memory_space=pl.ANY)


def times_rows(left, right):
    return lax.dot_general(
        left, right, (((1,), (1,)), ((), ())), preferred_element_type=jnp.float32
    )


def swap(value, axis, mask):
    count = lax.axis_size(axis)
    return lax.ppermute(value, axis, [(i, i ^ mask) for i in range(count)])


def send(value, step):
    return swap(value.astype(jnp.bfloat16), *step)


def wide(value):
    return value.astype(jnp.float32)


def squares():
    plane = [1 << bit for bit in range(1, lax.axis_size("dp").bit_length() - 1)]
    x_masks, y_masks = plane[: len(plane) // 2], plane[len(plane) // 2 :]
    return [(("dp", x), ("dp", y)) for x, y in zip(x_masks, y_masks)]


CORE = ("dp", 1)


def cat(parts):
    return parts[0] if len(parts) == 1 else jnp.concatenate(parts)


def split(value, count):
    step = value.shape[0] // count
    return [value[start : start + step] for start in range(0, value.shape[0], step)]


def gather_rows(block, loads):
    depth = lax.axis_size("expert")
    column = [block] + [swap(block, "expert", mask) for mask in range(1, depth)]
    near = cat(column[: depth // 2])
    near, *column = lax.optimization_barrier((near, *column[depth // 2 :]))
    far = cat(column)
    held = [hold(*loads[0])]
    far, *held = lax.optimization_barrier((far, *held))
    levels = squares()
    for level, (x, y) in enumerate(levels):
        near_x, near_y = swap(near, *x), swap(near, *y)
        far_x, far_y = swap(far, *x), swap(far, *y)
        if level == 0:
            expert, *weights = loads[1]
            near_x, *weights = lax.optimization_barrier((near_x, *weights))
            far_y, *held = lax.optimization_barrier((far_y, *held, hold(expert, *weights)))
        near_d, far_d = swap(near_x, *y), swap(far_y, *x)
        if level < len(levels) - 1:
            near, far = cat([near, near_x, near_y, near_d]), cat([far, far_x, far_y, far_d])
    groups = [cat([near, far]), cat([near_x, near_y, far_x, far_y]), cat([near_d, far_d])]
    return groups, [swap(group, *CORE) for group in groups], held


def scatter_sums(kept, away):
    def joined(index):
        return kept[index] + swap(away[index], *CORE).astype(jnp.float32)

    near_d, far_d = split(joined(2), 2)
    near_x, near_y, far_x, far_y = split(joined(1), 4)
    near, far = split(joined(0), 2)
    levels = squares()[::-1]
    for level, (x, y) in enumerate(levels):
        if level > 0:
            near, near_x, near_y, near_d = split(near, 4)
            far, far_x, far_y, far_d = split(far, 4)
        far_d_here, far_x_here = send(far_d, x), send(far_x, x)
        near_d_here, near_y_here = send(near_d, y), send(near_y, y)
        far_y_here = send(far_y + wide(far_d_here), y)
        near_x_here = send(near_x + wide(near_d_here), x)
        far = far + wide(far_x_here) + wide(far_y_here)
        far, near_x_here, near_y_here = lax.optimization_barrier((far, near_x_here, near_y_here))
        near = near + wide(near_y_here) + wide(near_x_here)
    depth = lax.axis_size("expert")
    total, *column = split(near, depth // 2) + split(far, depth // 2)
    for mask in range(depth - 1, 0, -1):
        total = total + wide(send(column[mask - 1], ("expert", mask)))
    return total.astype(jnp.bfloat16)


def pack_kernel(tokens_hbm, ids_hbm, router_hbm, packed_ref, tokens_ref, ids_ref, router_ref, done):
    pairs = [(tokens_hbm, tokens_ref), (ids_hbm, ids_ref), (router_hbm, router_ref)]
    copies = [
        pltpu.make_async_copy(source, target, done.at[index])
        for index, (source, target) in enumerate(pairs)
    ]
    for copy in copies:
        copy.start()
    for copy in copies:
        copy.wait()
    tokens = tokens_ref[...]
    width, expert_total = tokens.shape[1], router_ref.shape[0]
    logits = times_rows(tokens, router_ref[...])
    experts = lax.broadcasted_iota(jnp.int32, logits.shape, 1)
    ids = ids_ref[...]
    chosen = experts < 0
    for pick in range(ids.shape[1]):
        chosen = jnp.logical_or(chosen, ids[:, pick : pick + 1] == experts)
    scores = jnp.where(chosen, 1.0 / (1.0 + jnp.exp(-logits)), 0.0)
    rest = scores / jnp.sum(scores, axis=1, keepdims=True)
    place = (expert_total, packed_ref.shape[1] - width)
    source, lane = [lax.broadcasted_iota(jnp.int32, place, axis) for axis in (0, 1)]
    tags = 0.0
    for term in range(TERMS):
        part = rest.astype(jnp.bfloat16)
        rest = rest - part.astype(jnp.float32)
        moved = (lane == source + term * expert_total).astype(jnp.float32).astype(jnp.bfloat16)
        tags = tags + jnp.dot(part, moved, preferred_element_type=jnp.float32)
    packed_ref[:, :width] = tokens
    packed_ref[:, width:] = tags.astype(jnp.bfloat16)


def pack(tokens, expert_ids, router):
    rows, width = tokens.shape
    extra = -(-TERMS * router.shape[0] // LANES) * LANES
    return pl.pallas_call(
        pack_kernel,
        out_shape=pltpu.VMEM((rows, width + extra), tokens.dtype),
        in_specs=[ANYWHERE] * 3,
        out_specs=IN_VMEM,
        scratch_shapes=[
            *[pltpu.VMEM(value.shape, value.dtype) for value in (tokens, expert_ids, router)],
            pltpu.SemaphoreType.DMA((3,)),
        ],
        cost_estimate=pl.CostEstimate(
            flops=2 * rows * router.size, bytes_accessed=4 * router.size, transcendentals=0
        ),
    )(*[pltpu.with_memory_space_constraint(v, pltpu.HBM) for v in (tokens, expert_ids, router)])


def load_kernel(expert, *refs):
    *sources, held_ref, done = refs
    units = sources[0].shape[1]
    step = units // COPIES
    copies = [
        pltpu.make_async_copy(
            source.at[expert, pl.ds(part * step, step)],
            held_ref.at[pl.ds(index * units + part * step, step)],
            done.at[index * COPIES + part],
        )
        for index, source in enumerate(sources)
        for part in range(COPIES)
    ]
    for copy in copies:
        copy.start()
    for copy in copies:
        copy.wait()


def hold(expert, *weights):
    _, units, width = weights[0].shape
    return pl.pallas_call(
        functools.partial(load_kernel, expert),
        out_shape=pltpu.VMEM((len(weights) * units, width), weights[0].dtype),
        in_specs=[ANYWHERE] * len(weights),
        out_specs=IN_VMEM,
        scratch_shapes=[pltpu.SemaphoreType.DMA((len(weights) * COPIES,))],
        compiler_params=pltpu.CompilerParams(vmem_limit_bytes=1024 * 1024),
        cost_estimate=pl.CostEstimate(flops=0, bytes_accessed=0, transcendentals=0),
    )(*[pltpu.with_memory_space_constraint(weight, pltpu.HBM) for weight in weights])


def expert_kernel(exp_dev, expert_total, parts, *refs):
    pieces, refs = refs[:parts], refs[parts:]
    held, down_hbm, refs = refs[:exp_dev], refs[exp_dev], refs[exp_dev + 1 :]
    results, (rows_ref, down_ref, down_done) = refs[:parts], refs[parts:]
    units, width = down_ref.shape[1:]
    step = units // COPIES
    loads = [
        pltpu.make_async_copy(
            down_hbm.at[local, pl.ds(part * step, step)],
            down_ref.at[local, pl.ds(part * step, step)],
            down_done.at[local * COPIES + part],
        )
        for local in range(exp_dev)
        for part in range(COPIES)
    ]
    for load in loads:
        load.start()
    spans, start = [], 0
    for piece in pieces:
        spans.append((start, start + piece.shape[0]))
        rows_ref[start : start + piece.shape[0]] = piece[...]
        start += piece.shape[0]
    tags = rows_ref[:, width:].astype(jnp.float32)
    lane = lax.rem(lax.broadcasted_iota(jnp.int32, tags.shape, 1), expert_total)
    first_expert = lax.axis_index("dp") * exp_dev
    hidden, shares = [], []
    for local in range(exp_dev):
        both = times_rows(held[local][...], rows_ref[:, :width])
        gate, up = both[:units], both[units:]
        gated = gate / (1.0 + jnp.exp(-gate)) * up
        hidden.append(gated.T.astype(jnp.bfloat16))
        mine = jnp.where(lane == first_expert + local, tags, 0.0)
        shares.append(jnp.sum(mine, axis=1, keepdims=True))
    for load in loads:
        load.wait()
    block = min(512, width)

    @pl.loop(0, width // block)
    def _(index):
        columns = pl.ds(pl.multiple_of(index * block, block), block)
        total = 0.0
        for local in range(exp_dev):
            out = jnp.dot(
                hidden[local], down_ref[local, :, columns], preferred_element_type=jnp.float32
            )
            total = total + out * shares[local]
        for (start, stop), result in zip(spans, results):
            result[:, columns] = total[start:stop].astype(result.dtype)


def run_experts(pieces, kinds, expert_total, held, w_down):
    exp_dev, units, width = w_down.shape
    rows = sum(piece.shape[0] for piece in pieces)
    held = [pltpu.with_memory_space_constraint(weight, pltpu.VMEM) for weight in held]
    down = pltpu.with_memory_space_constraint(w_down, pltpu.HBM)
    place = pltpu.VMEM if len(pieces) > 1 else jax.ShapeDtypeStruct
    return pl.pallas_call(
        functools.partial(expert_kernel, exp_dev, expert_total, len(pieces)),
        out_shape=[
            place((piece.shape[0], width), kind) for piece, kind in zip(pieces, kinds)
        ],
        in_specs=[IN_VMEM] * (len(pieces) + exp_dev) + [ANYWHERE],
        out_specs=[IN_VMEM] * len(pieces),
        scratch_shapes=[
            pltpu.VMEM((rows, pieces[0].shape[1]), jnp.bfloat16),
            pltpu.VMEM(w_down.shape, w_down.dtype),
            pltpu.SemaphoreType.DMA((exp_dev * COPIES,)),
        ],
        compiler_params=pltpu.CompilerParams(vmem_limit_bytes=VMEM_BYTES),
        cost_estimate=pl.CostEstimate(
            flops=6 * rows * exp_dev * units * width,
            bytes_accessed=rows * width * 5,
            transcendentals=rows * exp_dev * units,
        ),
    )(*pieces, *held, down)


def body(tokens, expert_ids, router, w_gate, w_up, w_down):
    loads = [(expert, w_gate, w_up) for expert in range(w_gate.shape[0])]
    here, there, held = gather_rows(pack(tokens, expert_ids, router), loads)
    pieces = here + there
    kinds = [jnp.float32] * len(here) + [jnp.bfloat16] * len(there)
    operands = (router.shape[0], held, w_down)
    if sum(piece.shape[0] for piece in pieces) <= ROWS:
        results = run_experts(pieces, kinds, *operands)
    else:
        results = []
        for piece, kind in zip(pieces, kinds):
            chunks = [
                run_experts([piece[start : start + ROWS]], [kind], *operands)[0]
                for start in range(0, piece.shape[0], ROWS)
            ]
            results.append(cat(chunks))
    return scatter_sums(results[: len(here)], results[len(here) :])


def solution(mesh):
    in_specs = (
        P(("dp", "expert"), None),
        P(("dp", "expert"), None),
        P(),
        P("dp", "expert", None),
        P("dp", "expert", None),
        P("dp", "expert", None),
    )
    out_specs = P(("dp", "expert"), None)
    return jax.shard_map(body, mesh=mesh, in_specs=in_specs, out_specs=out_specs, check_vma=False)
```

```python
import functools

import jax
import jax.numpy as jnp
from jax import lax
from jax.experimental import pallas as pl
from jax.experimental.pallas import tpu as pltpu
from jax.sharding import PartitionSpec as P

LANES = 128
ROWS = 256
COPIES = 4
TERMS = 3
VMEM_BYTES = 36 * 1024 * 1024
IN_VMEM = pl.BlockSpec(memory_space=pltpu.VMEM)
ANYWHERE = pl.BlockSpec(memory_space=pl.ANY)


def times_rows(left, right):
    return lax.dot_general(
        left, right, (((1,), (1,)), ((), ())), preferred_element_type=jnp.float32
    )


def swap(value, axis, masks):
    count = lax.axis_size(axis)
    perm = [(i, i ^ masks[i % len(masks)]) for i in range(count)]
    return lax.ppermute(value, axis, perm)


def send(value, step):
    return swap(value.astype(jnp.bfloat16), *step)


def wide(value):
    return value.astype(jnp.float32)


CORE = ("dp", (1,))


def plane_steps():
    bits = [1 << bit for bit in range(1, lax.axis_size("dp").bit_length() - 1)]
    steps = []
    for x, y in zip(bits[: len(bits) // 2], bits[len(bits) // 2 :]):
        steps += [("dp", (x, y)), ("dp", (y, x))]
    return steps


def cat(parts):
    return parts[0] if len(parts) == 1 else jnp.concatenate(parts)


def split(value, count):
    step = value.shape[0] // count
    return [value[start : start + step] for start in range(0, value.shape[0], step)]


def gather_rows(block, load):
    depth = lax.axis_size("expert")
    column = [block] + [swap(block, "expert", (mask,)) for mask in range(1, depth)]
    *steps, last = plane_steps()
    near = cat(column[: depth // 2])
    far, held = lax.optimization_barrier((cat(column[depth // 2 :]), hold(*load)))
    near_here, far_here = swap(near, *steps[0]), swap(far, *steps[0])
    near, far = cat([near, near_here]), cat([far, far_here])
    for step in steps[1:]:
        near, far = cat([near, swap(near, *step)]), cat([far, swap(far, *step)])
    near_tail, far_tail = swap(near, *last), swap(far, *last)
    near_tail, far = lax.optimization_barrier((near_tail, far))
    near = cat([near, near_tail])
    far_tail, near_there = lax.optimization_barrier((far_tail, swap(near, *CORE)))
    far = cat([far, far_tail])
    return [near, far, near_there, swap(far, *CORE)], held


def scatter_sums(kept, away):
    near_kept, (far_kept, tail_kept) = kept[0], split(kept[1], 2)
    tail = tail_kept + wide(swap(away[2], *CORE))
    near, near_tail = split(near_kept + wide(swap(away[0], *CORE)), 2)
    far = far_kept + wide(swap(away[1], *CORE))
    *steps, last = plane_steps()
    for index, step in enumerate([last] + steps[::-1]):
        if index > 0:
            far, tail = split(far, 2)
        far_here = send(tail, step)
        if index > 0:
            far_here, near = lax.optimization_barrier((far_here, near))
            near, near_tail = split(near, 2)
        near, far = near + wide(send(near_tail, step)), far + wide(far_here)
    depth = lax.axis_size("expert")
    total, *column = split(near, depth // 2) + split(far, depth // 2)
    column = [send(part, ("expert", (mask + 1,))) for mask, part in enumerate(column)]
    near_column, far_column = column[: depth // 2 - 1], column[depth // 2 - 1 :]
    far = sum(wide(part) for part in far_column)
    far, *near_column = lax.optimization_barrier((far, *near_column))
    return sum([wide(part) for part in near_column], total + far).astype(jnp.bfloat16)


def pack_kernel(tokens_hbm, ids_hbm, router_hbm, packed_ref, tokens_ref, ids_ref, router_ref, done):
    pairs = [(tokens_hbm, tokens_ref), (ids_hbm, ids_ref), (router_hbm, router_ref)]
    copies = [
        pltpu.make_async_copy(source, target, done.at[index])
        for index, (source, target) in enumerate(pairs)
    ]
    for copy in copies:
        copy.start()
    for copy in copies:
        copy.wait()
    tokens = tokens_ref[...]
    width, expert_total = tokens.shape[1], router_ref.shape[0]
    logits = times_rows(tokens, router_ref[...])
    experts = lax.broadcasted_iota(jnp.int32, logits.shape, 1)
    ids = ids_ref[...]
    chosen = experts < 0
    for pick in range(ids.shape[1]):
        chosen = jnp.logical_or(chosen, ids[:, pick : pick + 1] == experts)
    scores = jnp.where(chosen, 1.0 / (1.0 + jnp.exp(-logits)), 0.0)
    rest = scores / jnp.sum(scores, axis=1, keepdims=True)
    place = (expert_total, packed_ref.shape[1] - width)
    source, lane = [lax.broadcasted_iota(jnp.int32, place, axis) for axis in (0, 1)]
    tags = 0.0
    for term in range(TERMS):
        part = rest.astype(jnp.bfloat16)
        rest = rest - part.astype(jnp.float32)
        moved = (lane == source + term * expert_total).astype(jnp.float32).astype(jnp.bfloat16)
        tags = tags + jnp.dot(part, moved, preferred_element_type=jnp.float32)
    packed_ref[:, :width] = tokens
    packed_ref[:, width:] = tags.astype(jnp.bfloat16)


def pack(tokens, expert_ids, router):
    rows, width = tokens.shape
    extra = -(-TERMS * router.shape[0] // LANES) * LANES
    return pl.pallas_call(
        pack_kernel,
        out_shape=pltpu.VMEM((rows, width + extra), tokens.dtype),
        in_specs=[ANYWHERE] * 3,
        out_specs=IN_VMEM,
        scratch_shapes=[
            *[pltpu.VMEM(value.shape, value.dtype) for value in (tokens, expert_ids, router)],
            pltpu.SemaphoreType.DMA((3,)),
        ],
        cost_estimate=pl.CostEstimate(
            flops=2 * rows * router.size, bytes_accessed=4 * router.size, transcendentals=0
        ),
    )(*[pltpu.with_memory_space_constraint(v, pltpu.HBM) for v in (tokens, expert_ids, router)])


def load_kernel(expert, *refs):
    *sources, held_ref, done = refs
    units = sources[0].shape[1]
    step = units // COPIES
    copies = [
        pltpu.make_async_copy(
            source.at[expert, pl.ds(part * step, step)],
            held_ref.at[pl.ds(index * units + part * step, step)],
            done.at[index * COPIES + part],
        )
        for index, source in enumerate(sources)
        for part in range(COPIES)
    ]
    for copy in copies:
        copy.start()
    for copy in copies:
        copy.wait()


def hold(expert, *weights):
    _, units, width = weights[0].shape
    return pl.pallas_call(
        functools.partial(load_kernel, expert),
        out_shape=pltpu.VMEM((len(weights) * units, width), weights[0].dtype),
        in_specs=[ANYWHERE] * len(weights),
        out_specs=IN_VMEM,
        scratch_shapes=[pltpu.SemaphoreType.DMA((len(weights) * COPIES,))],
        compiler_params=pltpu.CompilerParams(vmem_limit_bytes=1024 * 1024),
        cost_estimate=pl.CostEstimate(flops=0, bytes_accessed=0, transcendentals=0),
    )(*[pltpu.with_memory_space_constraint(weight, pltpu.HBM) for weight in weights])


def expert_kernel(exp_dev, expert_total, parts, *refs):
    pieces, refs = refs[:parts], refs[parts:]
    (held_ref, gate_hbm, up_hbm, down_hbm), refs = refs[:4], refs[4:]
    *results, rows_ref, both_ref, down_ref, done = refs
    units, width = down_ref.shape[1:]
    step = units // COPIES

    def copies(source, target, first):
        return [
            pltpu.make_async_copy(
                source.at[pl.ds(part * step, step)],
                target.at[pl.ds(part * step, step)],
                done.at[first + part],
            )
            for part in range(COPIES)
        ]

    loads, first = [[]], 0
    for local in range(1, exp_dev):
        loads.append([])
        for index, source in enumerate((gate_hbm, up_hbm)):
            target = both_ref.at[local - 1, pl.ds(index * units, units)]
            loads[local] += copies(source.at[local], target, first)
            first += COPIES
    down_loads = []
    for local in range(exp_dev):
        down_loads += copies(down_hbm.at[local], down_ref.at[local], first)
        first += COPIES
    for load in sum(loads, []) + down_loads:
        load.start()
    start = 0
    for piece in pieces:
        rows_ref[start : start + piece.shape[0]] = piece[...]
        start += piece.shape[0]
    tags = rows_ref[:, width:].astype(jnp.float32)
    lane = lax.rem(lax.broadcasted_iota(jnp.int32, tags.shape, 1), expert_total)
    first_expert = lax.axis_index("dp") * exp_dev
    hidden, shares = [], []
    for local in range(exp_dev):
        for load in loads[local]:
            load.wait()
        weights = held_ref[...] if local == 0 else both_ref[local - 1]
        both = times_rows(rows_ref[:, :width], weights)
        gate, up = both[:, :units], both[:, units:]
        hidden.append((gate / (1.0 + jnp.exp(-gate)) * up).astype(jnp.bfloat16))
        mine = jnp.where(lane == first_expert + local, tags, 0.0)
        shares.append(jnp.sum(mine, axis=1, keepdims=True))
    for load in down_loads:
        load.wait()
    block = min(512, width)

    @pl.loop(0, width // block)
    def _(index):
        columns = pl.ds(pl.multiple_of(index * block, block), block)
        total = 0.0
        for local in range(exp_dev):
            out = jnp.dot(
                hidden[local], down_ref[local, :, columns], preferred_element_type=jnp.float32
            )
            total = total + out * shares[local]
        start = 0
        for result in results:
            stop = start + result.shape[0]
            result[:, columns] = total[start:stop].astype(result.dtype)
            start = stop


def run_experts(pieces, shapes, expert_total, held, *weights):
    exp_dev, units, width = weights[0].shape
    rows = sum(piece.shape[0] for piece in pieces)
    held = pltpu.with_memory_space_constraint(held, pltpu.VMEM)
    weights = [pltpu.with_memory_space_constraint(weight, pltpu.HBM) for weight in weights]
    place = pltpu.VMEM if len(pieces) > 1 else jax.ShapeDtypeStruct
    return pl.pallas_call(
        functools.partial(expert_kernel, exp_dev, expert_total, len(pieces)),
        out_shape=[place((size, width), kind) for size, kind in shapes],
        in_specs=[IN_VMEM] * (len(pieces) + 1) + [ANYWHERE] * 3,
        out_specs=[IN_VMEM] * len(shapes),
        scratch_shapes=[
            pltpu.VMEM((rows, pieces[0].shape[1]), jnp.bfloat16),
            pltpu.VMEM((max(1, exp_dev - 1), 2 * units, width), jnp.bfloat16),
            pltpu.VMEM((exp_dev, units, width), jnp.bfloat16),
            pltpu.SemaphoreType.DMA(((3 * exp_dev - 2) * COPIES,)),
        ],
        compiler_params=pltpu.CompilerParams(vmem_limit_bytes=VMEM_BYTES),
        cost_estimate=pl.CostEstimate(
            flops=6 * rows * exp_dev * units * width,
            bytes_accessed=rows * width * 5,
            transcendentals=rows * exp_dev * units,
        ),
    )(*pieces, held, *weights)


def body(tokens, expert_ids, router, w_gate, w_up, w_down):
    pieces, held = gather_rows(pack(tokens, expert_ids, router), (0, w_gate, w_up))
    count = pieces[0].shape[0]
    shapes = [(count, jnp.float32)] * 2 + [(count, jnp.bfloat16)] + [(count // 2, jnp.bfloat16)] * 2
    operands = (router.shape[0], held, w_gate, w_up, w_down)
    if 4 * count <= ROWS:
        results = run_experts(pieces, shapes, *operands)
    else:
        rows, results, start = cat(pieces), [], 0
        for size, kind in shapes:
            chunks = [
                run_experts([rows[first : first + ROWS]], [(ROWS, kind)], *operands)[0]
                for first in range(start, start + size, ROWS)
            ]
            results.append(cat(chunks))
            start += size
    return scatter_sums(results[:2], results[2:])


def solution(mesh):
    in_specs = (
        P(("dp", "expert"), None),
        P(("dp", "expert"), None),
        P(),
        P("dp", "expert", None),
        P("dp", "expert", None),
        P("dp", "expert", None),
    )
    out_specs = P(("dp", "expert"), None)
    return jax.shard_map(body, mesh=mesh, in_specs=in_specs, out_specs=out_specs, check_vma=False)
```

```python
import functools

import jax
import jax.numpy as jnp
from jax import lax
from jax.experimental import pallas as pl
from jax.experimental.pallas import tpu as pltpu
from jax.sharding import PartitionSpec as P

LANES = 128
ROWS = 256
COPIES = 4
TERMS = 3
VMEM_BYTES = 30 * 1024 * 1024
IN_VMEM = pl.BlockSpec(memory_space=pltpu.VMEM)
ANYWHERE = pl.BlockSpec(memory_space=pl.ANY)


def times_rows(left, right):
    return lax.dot_general(
        left, right, (((1,), (1,)), ((), ())), preferred_element_type=jnp.float32
    )


def swap(value, axis, masks):
    count = lax.axis_size(axis)
    perm = [(i, i ^ masks[i % len(masks)]) for i in range(count)]
    return lax.ppermute(value, axis, perm)


def send(value, step):
    return swap(value.astype(jnp.bfloat16), *step)


def wide(value):
    return value.astype(jnp.float32)


CORE = ("dp", (1,))


def plane_steps():
    bits = [1 << bit for bit in range(1, lax.axis_size("dp").bit_length() - 1)]
    steps = []
    for x, y in zip(bits[: len(bits) // 2], bits[len(bits) // 2 :]):
        steps += [("dp", (x, y)), ("dp", (y, x))]
    return steps


def cat(parts):
    return parts[0] if len(parts) == 1 else jnp.concatenate(parts)


def split(value, count):
    step = value.shape[0] // count
    return [value[start : start + step] for start in range(0, value.shape[0], step)]


def gather_rows(block, w_gate, w_up, w_down):
    depth = lax.axis_size("expert")
    column = [block] + [swap(block, "expert", (mask,)) for mask in range(1, depth)]
    *steps, last = plane_steps()
    far, held = lax.optimization_barrier((cat(column[depth // 2 :]), hold(0, w_gate, w_up)))
    head = cat(column[: depth // 2] + [far])
    for step in steps:
        head = cat([head, swap(head, *step)])
    head, w_gate, w_up, w_down = lax.optimization_barrier((head, w_gate, w_up, w_down))
    tail = swap(head, *last)
    more = [hold(slot, w_gate, w_up) for slot in range(1, w_gate.shape[0])]
    ready, *more = lax.optimization_barrier((head, *more))
    tail, head_there, down = lax.optimization_barrier(
        (tail, swap(ready, *CORE), hold(None, w_down))
    )
    return [head, tail, head_there, swap(tail, *CORE)], [held, *more, down]


def scatter_sums(kept, away):
    (head, tail), (head_there, tail_there) = kept, away
    part = head + wide(swap(head_there, *CORE))
    tail = tail + wide(swap(tail_there, *CORE))
    *steps, last = plane_steps()
    part = part + wide(send(tail, last))
    for step in steps[::-1]:
        part, tail = split(part, 2)
        part = part + wide(send(tail, step))
    total, *column = split(part, lax.axis_size("expert"))
    for mask, part in enumerate(column):
        total = total + wide(send(part, ("expert", (mask + 1,))))
    return total.astype(jnp.bfloat16)


def pack_kernel(tokens_hbm, ids_hbm, router_hbm, packed_ref, tokens_ref, ids_ref, router_ref, done):
    pairs = [(tokens_hbm, tokens_ref), (ids_hbm, ids_ref), (router_hbm, router_ref)]
    copies = [
        pltpu.make_async_copy(source, target, done.at[index])
        for index, (source, target) in enumerate(pairs)
    ]
    for copy in copies:
        copy.start()
    for copy in copies:
        copy.wait()
    tokens = tokens_ref[...]
    width, expert_total = tokens.shape[1], router_ref.shape[0]
    logits = times_rows(tokens, router_ref[...])
    experts = lax.broadcasted_iota(jnp.int32, logits.shape, 1)
    ids = ids_ref[...]
    chosen = experts < 0
    for pick in range(ids.shape[1]):
        chosen = jnp.logical_or(chosen, ids[:, pick : pick + 1] == experts)
    scores = jnp.where(chosen, 1.0 / (1.0 + jnp.exp(-logits)), 0.0)
    rest = scores / jnp.sum(scores, axis=1, keepdims=True)
    place = (expert_total, packed_ref.shape[1] - width)
    source, lane = [lax.broadcasted_iota(jnp.int32, place, axis) for axis in (0, 1)]
    tags = 0.0
    for term in range(TERMS):
        part = rest.astype(jnp.bfloat16)
        rest = rest - part.astype(jnp.float32)
        moved = (lane == source + term * expert_total).astype(jnp.float32).astype(jnp.bfloat16)
        tags = tags + jnp.dot(part, moved, preferred_element_type=jnp.float32)
    packed_ref[:, :width] = tokens
    packed_ref[:, width:] = tags.astype(jnp.bfloat16)


def pack(tokens, expert_ids, router):
    rows, width = tokens.shape
    extra = -(-TERMS * router.shape[0] // LANES) * LANES
    return pl.pallas_call(
        pack_kernel,
        out_shape=pltpu.VMEM((rows, width + extra), tokens.dtype),
        in_specs=[ANYWHERE] * 3,
        out_specs=IN_VMEM,
        scratch_shapes=[
            *[pltpu.VMEM(value.shape, value.dtype) for value in (tokens, expert_ids, router)],
            pltpu.SemaphoreType.DMA((3,)),
        ],
        cost_estimate=pl.CostEstimate(
            flops=2 * rows * router.size, bytes_accessed=4 * router.size, transcendentals=0
        ),
    )(*[pltpu.with_memory_space_constraint(v, pltpu.HBM) for v in (tokens, expert_ids, router)])


def load_kernel(*refs):
    *sources, held_ref, done = refs
    units = held_ref.shape[0] // len(sources)
    step = units // COPIES
    copies = [
        pltpu.make_async_copy(
            source.at[pl.ds(part * step, step)],
            held_ref.at[pl.ds(index * units + part * step, step)],
            done.at[index * COPIES + part],
        )
        for index, source in enumerate(sources)
        for part in range(COPIES)
    ]
    for copy in copies:
        copy.start()
    for copy in copies:
        copy.wait()


def hold_kernel(slot, weights, *refs):
    sources, refs = refs[:weights], refs[weights:]
    if slot is None:
        parts = [source.at[index] for source in sources for index in range(source.shape[0])]
    else:
        parts = [source.at[slot] for source in sources]
    load_kernel(*parts, *refs)


def hold(slot, *weights):
    exp_dev, units, width = weights[0].shape
    parts = len(weights) * (exp_dev if slot is None else 1)
    return pl.pallas_call(
        functools.partial(hold_kernel, slot, len(weights)),
        out_shape=pltpu.VMEM((parts * units, width), weights[0].dtype),
        in_specs=[ANYWHERE] * len(weights),
        out_specs=IN_VMEM,
        scratch_shapes=[pltpu.SemaphoreType.DMA((parts * COPIES,))],
        compiler_params=pltpu.CompilerParams(vmem_limit_bytes=1024 * 1024),
        cost_estimate=pl.CostEstimate(flops=0, bytes_accessed=0, transcendentals=0),
    )(*[pltpu.with_memory_space_constraint(weight, pltpu.HBM) for weight in weights])


def expert_kernel(exp_dev, expert_total, parts, *refs):
    pieces, held, refs = refs[:parts], refs[parts : parts + exp_dev], refs[parts + exp_dev :]
    down_ref, *results, rows_ref = refs
    width = down_ref.shape[1]
    units = down_ref.shape[0] // exp_dev
    start = 0
    for piece in pieces:
        rows_ref[start : start + piece.shape[0]] = piece[...]
        start += piece.shape[0]
    tags = rows_ref[:, width:].astype(jnp.float32)
    lane = lax.rem(lax.broadcasted_iota(jnp.int32, tags.shape, 1), expert_total)
    first_expert = lax.axis_index("dp") * exp_dev
    hidden, shares = [], []
    for local in range(exp_dev):
        both = times_rows(rows_ref[:, :width], held[local][...])
        gate, up = both[:, :units], both[:, units:]
        hidden.append((gate / (1.0 + jnp.exp(-gate)) * up).astype(jnp.bfloat16))
        mine = jnp.where(lane == first_expert + local, tags, 0.0)
        shares.append(jnp.sum(mine, axis=1, keepdims=True))
    block = min(512, width)

    @pl.loop(0, width // block)
    def _(index):
        columns = pl.ds(pl.multiple_of(index * block, block), block)
        total = 0.0
        for local in range(exp_dev):
            out = jnp.dot(
                hidden[local],
                down_ref[pl.ds(local * units, units), columns],
                preferred_element_type=jnp.float32,
            )
            total = total + out * shares[local]
        start = 0
        for result in results:
            stop = start + result.shape[0]
            result[:, columns] = total[start:stop].astype(result.dtype)
            start = stop


def run_experts(pieces, kinds, expert_total, held):
    rows = sum(piece.shape[0] for piece in pieces)
    *both, down = [pltpu.with_memory_space_constraint(weight, pltpu.VMEM) for weight in held]
    exp_dev, width = len(both), down.shape[1]
    place = pltpu.VMEM if len(pieces) > 1 else jax.ShapeDtypeStruct
    return pl.pallas_call(
        functools.partial(expert_kernel, exp_dev, expert_total, len(pieces)),
        out_shape=[
            place((piece.shape[0], width), kind) for piece, kind in zip(pieces, kinds)
        ],
        in_specs=[IN_VMEM] * (len(pieces) + len(held)),
        out_specs=[IN_VMEM] * len(pieces),
        scratch_shapes=[pltpu.VMEM((rows, pieces[0].shape[1]), jnp.bfloat16)],
        compiler_params=pltpu.CompilerParams(vmem_limit_bytes=VMEM_BYTES),
        cost_estimate=pl.CostEstimate(
            flops=6 * rows * down.size, bytes_accessed=rows * width * 5, transcendentals=0
        ),
    )(*pieces, *both, down)


def body(tokens, expert_ids, router, w_gate, w_up, w_down):
    pieces, held = gather_rows(pack(tokens, expert_ids, router), w_gate, w_up, w_down)
    kinds = [jnp.float32] * 2 + [jnp.bfloat16] * 2
    operands = (router.shape[0], held)
    count = pieces[0].shape[0]
    if 4 * count <= ROWS:
        results = run_experts(pieces, kinds, *operands)
    else:
        results = []
        for piece, kind in zip(pieces, kinds):
            chunks = [
                run_experts([piece[start : start + ROWS]], [kind], *operands)[0]
                for start in range(0, count, ROWS)
            ]
            results.append(cat(chunks))
    return scatter_sums(results[:2], results[2:])


def solution(mesh):
    in_specs = (
        P(("dp", "expert"), None),
        P(("dp", "expert"), None),
        P(),
        P("dp", "expert", None),
        P("dp", "expert", None),
        P("dp", "expert", None),
    )
    out_specs = P(("dp", "expert"), None)
    return jax.shard_map(body, mesh=mesh, in_specs=in_specs, out_specs=out_specs, check_vma=False)
```

```python
import functools

import jax
import jax.numpy as jnp
from jax import lax
from jax.experimental import pallas as pl
from jax.experimental.pallas import tpu as pltpu
from jax.sharding import PartitionSpec as P

LANES = 128
ROWS = 256
COPIES = 4
TERMS = 3
VMEM_BYTES = 30 * 1024 * 1024
IN_VMEM = pl.BlockSpec(memory_space=pltpu.VMEM)
ANYWHERE = pl.BlockSpec(memory_space=pl.ANY)


def times_rows(left, right):
    return lax.dot_general(
        left, right, (((1,), (1,)), ((), ())), preferred_element_type=jnp.float32
    )


def swap(value, axis, mask):
    count = lax.axis_size(axis)
    return lax.ppermute(value, axis, [(i, i ^ mask) for i in range(count)])


def send(value, step):
    return swap(value.astype(jnp.bfloat16), *step)


def wide(value):
    return value.astype(jnp.float32)


CORE = ("dp", 1)


def plane_steps():
    return [("dp", mask) for mask in range(lax.axis_size("dp") - 2, 0, -2)]


def cat(parts):
    return parts[0] if len(parts) == 1 else jnp.concatenate(parts)


def split(value, count):
    step = value.shape[0] // count
    return [value[start : start + step] for start in range(0, value.shape[0], step)]


def gather_rows(block, w_gate, w_up, w_down):
    depth = lax.axis_size("expert")
    column = [block] + [swap(block, "expert", mask) for mask in range(1, depth)]
    near, column = cat(column[: depth // 2]), column[depth // 2 :]
    near, w_gate, w_up, w_down = lax.optimization_barrier((near, w_gate, w_up, w_down))
    near_rest = [swap(near, *step) for step in plane_steps()]
    held = hold(0, w_gate, w_up)
    held, *column = lax.optimization_barrier((held, *column))
    far = cat(column)
    far, w_gate, w_up, w_down = lax.optimization_barrier((far, w_gate, w_up, w_down))
    far_rest = [swap(far, *step) for step in plane_steps()]
    more = [hold(slot, w_gate, w_up) for slot in range(1, w_gate.shape[0])]
    count = len(near_rest)
    far_rest[0], *rest = lax.optimization_barrier((far_rest[0], *near_rest, *more))
    near_rest, more = rest[:count], rest[count:]
    near = cat([near, *near_rest])
    near_there, down, *far_rest = lax.optimization_barrier(
        (swap(near, *CORE), hold(None, w_down), *far_rest)
    )
    far = cat([far, *far_rest])
    return [near, far, near_there, swap(far, *CORE)], [held, *more, down]


def scatter_sums(kept, away):
    steps, depth = plane_steps(), lax.axis_size("expert")
    sums = []
    for mine, other in reversed(list(zip(kept, away))):
        part, *rest = split(mine + wide(swap(other, *CORE)), len(steps) + 1)
        here = [send(other, step) for other, step in zip(rest, steps)]
        sums.append(sum([wide(other) for other in here], part))
    far, (total, *near) = split(sums[0], depth // 2), split(sums[1], depth // 2)
    far = [send(part, ("expert", mask + depth // 2)) for mask, part in enumerate(far)]
    near = [send(part, ("expert", mask + 1)) for mask, part in enumerate(near)]
    far = sum(wide(part) for part in far)
    far, *near = lax.optimization_barrier((far, *near))
    return sum([wide(part) for part in near], total + far).astype(jnp.bfloat16)


def pack_kernel(tokens_hbm, ids_hbm, router_hbm, packed_ref, tokens_ref, ids_ref, router_ref, done):
    pairs = [(tokens_hbm, tokens_ref), (ids_hbm, ids_ref), (router_hbm, router_ref)]
    copies = [
        pltpu.make_async_copy(source, target, done.at[index])
        for index, (source, target) in enumerate(pairs)
    ]
    for copy in copies:
        copy.start()
    for copy in copies:
        copy.wait()
    tokens = tokens_ref[...]
    width, expert_total = tokens.shape[1], router_ref.shape[0]
    logits = times_rows(tokens, router_ref[...])
    experts = lax.broadcasted_iota(jnp.int32, logits.shape, 1)
    ids = ids_ref[...]
    chosen = experts < 0
    for pick in range(ids.shape[1]):
        chosen = jnp.logical_or(chosen, ids[:, pick : pick + 1] == experts)
    scores = jnp.where(chosen, 1.0 / (1.0 + jnp.exp(-logits)), 0.0)
    rest = scores / jnp.sum(scores, axis=1, keepdims=True)
    place = (expert_total, packed_ref.shape[1] - width)
    source, lane = [lax.broadcasted_iota(jnp.int32, place, axis) for axis in (0, 1)]
    tags = 0.0
    for term in range(TERMS):
        part = rest.astype(jnp.bfloat16)
        rest = rest - part.astype(jnp.float32)
        moved = (lane == source + term * expert_total).astype(jnp.float32).astype(jnp.bfloat16)
        tags = tags + jnp.dot(part, moved, preferred_element_type=jnp.float32)
    packed_ref[:, :width] = tokens
    packed_ref[:, width:] = tags.astype(jnp.bfloat16)


def pack(tokens, expert_ids, router):
    rows, width = tokens.shape
    extra = -(-TERMS * router.shape[0] // LANES) * LANES
    return pl.pallas_call(
        pack_kernel,
        out_shape=pltpu.VMEM((rows, width + extra), tokens.dtype),
        in_specs=[ANYWHERE] * 3,
        out_specs=IN_VMEM,
        scratch_shapes=[
            *[pltpu.VMEM(value.shape, value.dtype) for value in (tokens, expert_ids, router)],
            pltpu.SemaphoreType.DMA((3,)),
        ],
        cost_estimate=pl.CostEstimate(
            flops=2 * rows * router.size, bytes_accessed=4 * router.size, transcendentals=0
        ),
    )(*[pltpu.with_memory_space_constraint(v, pltpu.HBM) for v in (tokens, expert_ids, router)])


def load_kernel(*refs):
    *sources, held_ref, done = refs
    units = held_ref.shape[0] // len(sources)
    step = units // COPIES
    copies = [
        pltpu.make_async_copy(
            source.at[pl.ds(part * step, step)],
            held_ref.at[pl.ds(index * units + part * step, step)],
            done.at[index * COPIES + part],
        )
        for index, source in enumerate(sources)
        for part in range(COPIES)
    ]
    for copy in copies:
        copy.start()
    for copy in copies:
        copy.wait()


def hold_kernel(slot, weights, *refs):
    sources, refs = refs[:weights], refs[weights:]
    if slot is None:
        parts = [source.at[index] for source in sources for index in range(source.shape[0])]
    else:
        parts = [source.at[slot] for source in sources]
    load_kernel(*parts, *refs)


def hold(slot, *weights):
    exp_dev, units, width = weights[0].shape
    parts = len(weights) * (exp_dev if slot is None else 1)
    return pl.pallas_call(
        functools.partial(hold_kernel, slot, len(weights)),
        out_shape=pltpu.VMEM((parts * units, width), weights[0].dtype),
        in_specs=[ANYWHERE] * len(weights),
        out_specs=IN_VMEM,
        scratch_shapes=[pltpu.SemaphoreType.DMA((parts * COPIES,))],
        compiler_params=pltpu.CompilerParams(vmem_limit_bytes=1024 * 1024),
        cost_estimate=pl.CostEstimate(flops=0, bytes_accessed=0, transcendentals=0),
    )(*[pltpu.with_memory_space_constraint(weight, pltpu.HBM) for weight in weights])


def expert_kernel(exp_dev, expert_total, parts, *refs):
    pieces, held, refs = refs[:parts], refs[parts : parts + exp_dev], refs[parts + exp_dev :]
    down_ref, *results, rows_ref = refs
    width = down_ref.shape[1]
    units = down_ref.shape[0] // exp_dev
    start = 0
    for piece in pieces:
        rows_ref[start : start + piece.shape[0]] = piece[...]
        start += piece.shape[0]
    tags = rows_ref[:, width:].astype(jnp.float32)
    lane = lax.rem(lax.broadcasted_iota(jnp.int32, tags.shape, 1), expert_total)
    first_expert = lax.axis_index("dp") * exp_dev
    hidden, shares = [], []
    for local in range(exp_dev):
        both = times_rows(rows_ref[:, :width], held[local][...])
        gate, up = both[:, :units], both[:, units:]
        hidden.append((gate / (1.0 + jnp.exp(-gate)) * up).astype(jnp.bfloat16))
        mine = jnp.where(lane == first_expert + local, tags, 0.0)
        shares.append(jnp.sum(mine, axis=1, keepdims=True))
    block = min(512, width)

    @pl.loop(0, width // block)
    def _(index):
        columns = pl.ds(pl.multiple_of(index * block, block), block)
        total = 0.0
        for local in range(exp_dev):
            out = jnp.dot(
                hidden[local],
                down_ref[pl.ds(local * units, units), columns],
                preferred_element_type=jnp.float32,
            )
            total = total + out * shares[local]
        start = 0
        for result in results:
            stop = start + result.shape[0]
            result[:, columns] = total[start:stop].astype(result.dtype)
            start = stop


def run_experts(pieces, kinds, expert_total, held):
    rows = sum(piece.shape[0] for piece in pieces)
    *both, down = [pltpu.with_memory_space_constraint(weight, pltpu.VMEM) for weight in held]
    exp_dev, width = len(both), down.shape[1]
    place = pltpu.VMEM if len(pieces) > 1 else jax.ShapeDtypeStruct
    return pl.pallas_call(
        functools.partial(expert_kernel, exp_dev, expert_total, len(pieces)),
        out_shape=[
            place((piece.shape[0], width), kind) for piece, kind in zip(pieces, kinds)
        ],
        in_specs=[IN_VMEM] * (len(pieces) + len(held)),
        out_specs=[IN_VMEM] * len(pieces),
        scratch_shapes=[pltpu.VMEM((rows, pieces[0].shape[1]), jnp.bfloat16)],
        compiler_params=pltpu.CompilerParams(vmem_limit_bytes=VMEM_BYTES),
        cost_estimate=pl.CostEstimate(
            flops=6 * rows * down.size, bytes_accessed=rows * width * 5, transcendentals=0
        ),
    )(*pieces, *both, down)


def body(tokens, expert_ids, router, w_gate, w_up, w_down):
    pieces, held = gather_rows(pack(tokens, expert_ids, router), w_gate, w_up, w_down)
    kinds = [jnp.float32] * 2 + [jnp.bfloat16] * 2
    operands = (router.shape[0], held)
    if sum(piece.shape[0] for piece in pieces) <= ROWS:
        results = run_experts(pieces, kinds, *operands)
    else:
        results = []
        for piece, kind in zip(pieces, kinds):
            chunks = [
                run_experts([piece[start : start + ROWS]], [kind], *operands)[0]
                for start in range(0, piece.shape[0], ROWS)
            ]
            results.append(cat(chunks))
    return scatter_sums(results[:2], results[2:])


def solution(mesh):
    in_specs = (
        P(("dp", "expert"), None),
        P(("dp", "expert"), None),
        P(),
        P("dp", "expert", None),
        P("dp", "expert", None),
        P("dp", "expert", None),
    )
    out_specs = P(("dp", "expert"), None)
    return jax.shard_map(body, mesh=mesh, in_specs=in_specs, out_specs=out_specs, check_vma=False)
```

```python
import functools

import jax
import jax.numpy as jnp
from jax import lax
from jax.experimental import pallas as pl
from jax.experimental.pallas import tpu as pltpu
from jax.sharding import PartitionSpec as P

LANES = 128
ROWS = 256
TERMS = 3
VMEM_BYTES = 30 * 1024 * 1024
EXCHANGE_FLOPS = 20_000_000_000
IN_VMEM = pl.BlockSpec(memory_space=pltpu.VMEM)
ANYWHERE = pl.BlockSpec(memory_space=pl.ANY)


def times_rows(left, right):
    return lax.dot_general(
        left, right, (((1,), (1,)), ((), ())), preferred_element_type=jnp.float32
    )


def swap(value, axis, mask):
    count = lax.axis_size(axis)
    return lax.ppermute(value, axis, [(i, i ^ mask) for i in range(count)])


def send(value, step):
    return swap(value.astype(jnp.bfloat16), *step)


def wide(value):
    return value.astype(jnp.float32)


CORE = ("dp", 1)


def plane_steps():
    return [("dp", mask) for mask in range(lax.axis_size("dp") - 2, 0, -2)]


def cat(parts):
    return parts[0] if len(parts) == 1 else jnp.concatenate(parts)


def split(value, count):
    step = value.shape[0] // count
    return [value[start : start + step] for start in range(0, value.shape[0], step)]


def gather_rows(block, w_gate, w_up, w_down):
    depth = lax.axis_size("expert")
    column = [block] + [swap(block, "expert", mask) for mask in range(1, depth)]
    near, column = cat(column[: depth // 2]), column[depth // 2 :]
    near_rest = [swap(near, *step) for step in plane_steps()]
    far = cat(column)
    far_rest = [swap(far, *step) for step in plane_steps()]
    near = cat([near, *near_rest])
    near_there = swap(near, *CORE)
    far = cat([far, *far_rest])
    return [near, far, near_there, swap(far, *CORE)], [w_gate, w_up, w_down]


def scatter_sums(kept, away):
    steps, depth = plane_steps(), lax.axis_size("expert")
    sums = []
    for mine, other in reversed(list(zip(kept, away))):
        part, *rest = split(mine + wide(swap(other, *CORE)), len(steps) + 1)
        here = [send(other, step) for other, step in zip(rest, steps)]
        sums.append(sum([wide(other) for other in here], part))
    far, (total, *near) = split(sums[0], depth // 2), split(sums[1], depth // 2)
    far = [send(part, ("expert", mask + depth // 2)) for mask, part in enumerate(far)]
    near = [send(part, ("expert", mask + 1)) for mask, part in enumerate(near)]
    far = sum(wide(part) for part in far)
    far, *near = lax.optimization_barrier((far, *near))
    return sum([wide(part) for part in near], total + far).astype(jnp.bfloat16)


def pack_kernel(tokens_hbm, ids_hbm, router_hbm, packed_ref, tokens_ref, ids_ref, router_ref, done):
    pairs = [(tokens_hbm, tokens_ref), (ids_hbm, ids_ref), (router_hbm, router_ref)]
    copies = [
        pltpu.make_async_copy(source, target, done.at[index])
        for index, (source, target) in enumerate(pairs)
    ]
    for copy in copies:
        copy.start()
    for copy in copies:
        copy.wait()
    tokens = tokens_ref[...]
    width, expert_total = tokens.shape[1], router_ref.shape[0]
    logits = times_rows(tokens, router_ref[...])
    experts = lax.broadcasted_iota(jnp.int32, logits.shape, 1)
    ids = ids_ref[...]
    chosen = experts < 0
    for pick in range(ids.shape[1]):
        chosen = jnp.logical_or(chosen, ids[:, pick : pick + 1] == experts)
    scores = jnp.where(chosen, 1.0 / (1.0 + jnp.exp(-logits)), 0.0)
    rest = scores / jnp.sum(scores, axis=1, keepdims=True)
    place = (expert_total, packed_ref.shape[1] - width)
    source, lane = [lax.broadcasted_iota(jnp.int32, place, axis) for axis in (0, 1)]
    tags = 0.0
    for term in range(TERMS):
        part = rest.astype(jnp.bfloat16)
        rest = rest - part.astype(jnp.float32)
        moved = (lane == source + term * expert_total).astype(jnp.float32).astype(jnp.bfloat16)
        tags = tags + jnp.dot(part, moved, preferred_element_type=jnp.float32)
    packed_ref[:, :width] = tokens
    packed_ref[:, width:] = tags.astype(jnp.bfloat16)


def pack(tokens, expert_ids, router):
    rows, width = tokens.shape
    extra = -(-TERMS * router.shape[0] // LANES) * LANES
    return pl.pallas_call(
        pack_kernel,
        out_shape=pltpu.VMEM((rows, width + extra), tokens.dtype),
        in_specs=[ANYWHERE] * 3,
        out_specs=IN_VMEM,
        scratch_shapes=[
            *[pltpu.VMEM(value.shape, value.dtype) for value in (tokens, expert_ids, router)],
            pltpu.SemaphoreType.DMA((3,)),
        ],
        cost_estimate=pl.CostEstimate(
            flops=EXCHANGE_FLOPS, bytes_accessed=4 * router.size, transcendentals=0
        ),
    )(*[pltpu.with_memory_space_constraint(v, pltpu.HBM) for v in (tokens, expert_ids, router)])


def expert_kernel(exp_dev, expert_total, parts, *refs):
    pieces, (gate_ref, up_ref, down_ref, *results, rows_ref) = refs[:parts], refs[parts:]
    units, width = down_ref.shape[1:]
    start = 0
    for piece in pieces:
        rows_ref[start : start + piece.shape[0]] = piece[...]
        start += piece.shape[0]
    tags = rows_ref[:, width:].astype(jnp.float32)
    lane = lax.rem(lax.broadcasted_iota(jnp.int32, tags.shape, 1), expert_total)
    first_expert = lax.axis_index("dp") * exp_dev
    hidden, shares = [], []
    for local in range(exp_dev):
        weights = jnp.concatenate([gate_ref[local], up_ref[local]])
        both = times_rows(rows_ref[:, :width], weights)
        gate, up = both[:, :units], both[:, units:]
        hidden.append((gate / (1.0 + jnp.exp(-gate)) * up).astype(jnp.bfloat16))
        mine = jnp.where(lane == first_expert + local, tags, 0.0)
        shares.append(jnp.sum(mine, axis=1, keepdims=True))
    block = min(512, width)

    @pl.loop(0, width // block)
    def _(index):
        columns = pl.ds(pl.multiple_of(index * block, block), block)
        total = 0.0
        for local in range(exp_dev):
            out = jnp.dot(
                hidden[local],
                down_ref[local, :, columns],
                preferred_element_type=jnp.float32,
            )
            total = total + out * shares[local]
        start = 0
        for result in results:
            stop = start + result.shape[0]
            result[:, columns] = total[start:stop].astype(result.dtype)
            start = stop


def run_experts(pieces, kinds, expert_total, held):
    rows = sum(piece.shape[0] for piece in pieces)
    gate, up, down = held
    exp_dev, width = down.shape[0], down.shape[2]
    place = pltpu.VMEM if len(pieces) > 1 else jax.ShapeDtypeStruct
    return pl.pallas_call(
        functools.partial(expert_kernel, exp_dev, expert_total, len(pieces)),
        out_shape=[
            place((piece.shape[0], width), kind) for piece, kind in zip(pieces, kinds)
        ],
        in_specs=[IN_VMEM] * (len(pieces) + len(held)),
        out_specs=[IN_VMEM] * len(pieces),
        scratch_shapes=[pltpu.VMEM((rows, pieces[0].shape[1]), jnp.bfloat16)],
        compiler_params=pltpu.CompilerParams(vmem_limit_bytes=VMEM_BYTES),
        cost_estimate=pl.CostEstimate(
            flops=6 * rows * down.size, bytes_accessed=rows * width * 5, transcendentals=0
        ),
    )(*pieces, gate, up, down)


def body(tokens, expert_ids, router, w_gate, w_up, w_down):
    pieces, held = gather_rows(pack(tokens, expert_ids, router), w_gate, w_up, w_down)
    kinds = [jnp.float32] * 2 + [jnp.bfloat16] * 2
    operands = (router.shape[0], held)
    if sum(piece.shape[0] for piece in pieces) <= ROWS:
        results = run_experts(pieces, kinds, *operands)
    else:
        results = []
        for piece, kind in zip(pieces, kinds):
            chunks = [
                run_experts([piece[start : start + ROWS]], [kind], *operands)[0]
                for start in range(0, piece.shape[0], ROWS)
            ]
            results.append(cat(chunks))
    return scatter_sums(results[:2], results[2:])


def solution(mesh):
    in_specs = (
        P(("dp", "expert"), None),
        P(("dp", "expert"), None),
        P(),
        P("dp", "expert", None),
        P("dp", "expert", None),
        P("dp", "expert", None),
    )
    out_specs = P(("dp", "expert"), None)
    return jax.shard_map(body, mesh=mesh, in_specs=in_specs, out_specs=out_specs, check_vma=False)
```

```python
import functools

import jax
import jax.numpy as jnp
from jax import lax
from jax.experimental import pallas as pl
from jax.experimental.pallas import tpu as pltpu
from jax.sharding import PartitionSpec as P

LANES = 128
ROWS = 256
TERMS = 3
VMEM_BYTES = 24 * 1024 * 1024
SMALL_BYTES = 2 * 1024 * 1024
EXCHANGE_FLOPS = 20_000_000_000
IN_VMEM = pl.BlockSpec(memory_space=pltpu.VMEM)
ANYWHERE = pl.BlockSpec(memory_space=pl.ANY)


def times_rows(left, right):
    return lax.dot_general(
        left, right, (((1,), (1,)), ((), ())), preferred_element_type=jnp.float32
    )


def swap(value, axis, mask):
    count = lax.axis_size(axis)
    return lax.ppermute(value, axis, [(i, i ^ mask) for i in range(count)])


def send(value, step):
    return swap(value.astype(jnp.bfloat16), *step)


def wide(value):
    return value.astype(jnp.float32)


CORE = ("dp", 1)


def plane_steps():
    return [("dp", mask) for mask in range(lax.axis_size("dp") - 2, 0, -2)]


def cat(parts):
    return parts[0] if len(parts) == 1 else jnp.concatenate(parts)


def split(value, count):
    step = value.shape[0] // count
    return [value[start : start + step] for start in range(0, value.shape[0], step)]


def gather_rows(block):
    depth = lax.axis_size("expert")
    column = [block] + [swap(block, "expert", mask) for mask in range(1, depth)]
    near = join(column[: depth // 2])
    near_rest = [swap(near, *step) for step in plane_steps()]
    far = cat(column[depth // 2 :])
    far_rest = [swap(far, *step) for step in plane_steps()]
    near = cat([near, *near_rest])
    near_there = swap(near, *CORE)
    far = cat([far, *far_rest])
    return [near, far, near_there, swap(far, *CORE)]


def scatter_sums(kept, away):
    steps, depth = plane_steps(), lax.axis_size("expert")
    sums = []
    for mine, other in reversed(list(zip(kept, away))):
        part, *rest = split(mine + wide(swap(other, *CORE)), len(steps) + 1)
        here = [send(other, step) for other, step in zip(rest, steps)]
        sums.append(sum([wide(other) for other in here], part))
    far, (total, *near) = split(sums[0], depth // 2), split(sums[1], depth // 2)
    far = [send(part, ("expert", mask + depth // 2)) for mask, part in enumerate(far)]
    near = [send(part, ("expert", mask + 1)) for mask, part in enumerate(near)]
    far = sum(wide(part) for part in far)
    far, *near = lax.optimization_barrier((far, *near))
    return sum([wide(part) for part in near], total + far).astype(jnp.bfloat16)


def pack_kernel(tokens_hbm, ids_hbm, router_hbm, packed_ref, tokens_ref, ids_ref, router_ref, done):
    pairs = [(tokens_hbm, tokens_ref), (ids_hbm, ids_ref), (router_hbm, router_ref)]
    copies = [
        pltpu.make_async_copy(source, target, done.at[index])
        for index, (source, target) in enumerate(pairs)
    ]
    for copy in copies:
        copy.start()
    for copy in copies:
        copy.wait()
    tokens = tokens_ref[...]
    width, expert_total = tokens.shape[1], router_ref.shape[0]
    logits = times_rows(tokens, router_ref[...])
    experts = lax.broadcasted_iota(jnp.int32, logits.shape, 1)
    ids = ids_ref[...]
    chosen = experts < 0
    for pick in range(ids.shape[1]):
        chosen = jnp.logical_or(chosen, ids[:, pick : pick + 1] == experts)
    scores = jnp.where(chosen, 1.0 / (1.0 + jnp.exp(-logits)), 0.0)
    rest = scores / jnp.sum(scores, axis=1, keepdims=True)
    place = (expert_total, packed_ref.shape[1] - width)
    source, lane = [lax.broadcasted_iota(jnp.int32, place, axis) for axis in (0, 1)]
    tags = 0.0
    for term in range(TERMS):
        part = rest.astype(jnp.bfloat16)
        rest = rest - part.astype(jnp.float32)
        moved = (lane == source + term * expert_total).astype(jnp.float32).astype(jnp.bfloat16)
        tags = tags + jnp.dot(part, moved, preferred_element_type=jnp.float32)
    packed_ref[:, :width] = tokens
    packed_ref[:, width:] = tags.astype(jnp.bfloat16)


def pack(tokens, expert_ids, router):
    rows, width = tokens.shape
    extra = -(-TERMS * router.shape[0] // LANES) * LANES
    return pl.pallas_call(
        pack_kernel,
        out_shape=pltpu.VMEM((rows, width + extra), tokens.dtype),
        in_specs=[ANYWHERE] * 3,
        out_specs=IN_VMEM,
        scratch_shapes=[
            *[pltpu.VMEM(value.shape, value.dtype) for value in (tokens, expert_ids, router)],
            pltpu.SemaphoreType.DMA((3,)),
        ],
        compiler_params=pltpu.CompilerParams(vmem_limit_bytes=SMALL_BYTES),
        cost_estimate=pl.CostEstimate(
            flops=2 * rows * router.size, bytes_accessed=4 * router.size, transcendentals=0
        ),
    )(*[pltpu.with_memory_space_constraint(v, pltpu.HBM) for v in (tokens, expert_ids, router)])


def join_kernel(*refs):
    *parts, joined_ref = refs
    start = 0
    for part in parts:
        joined_ref[start : start + part.shape[0]] = part[...]
        start += part.shape[0]


def join(parts):
    rows, width = sum(part.shape[0] for part in parts), parts[0].shape[1]
    return pl.pallas_call(
        join_kernel,
        out_shape=pltpu.VMEM((rows, width), parts[0].dtype),
        in_specs=[IN_VMEM] * len(parts),
        out_specs=IN_VMEM,
        compiler_params=pltpu.CompilerParams(vmem_limit_bytes=SMALL_BYTES),
        cost_estimate=pl.CostEstimate(
            flops=EXCHANGE_FLOPS, bytes_accessed=0, transcendentals=0
        ),
    )(*parts)


def expert_kernel(exp_dev, expert_total, parts, *refs):
    pieces, refs = refs[:parts], refs[parts:]
    gate_ref, up_ref, down_ref, *results, rows_ref = refs
    units, width = down_ref.shape[1:]
    start = 0
    for piece in pieces:
        rows_ref[start : start + piece.shape[0]] = piece[...]
        start += piece.shape[0]
    tags = rows_ref[:, width:].astype(jnp.float32)
    lane = lax.rem(lax.broadcasted_iota(jnp.int32, tags.shape, 1), expert_total)
    first_expert = lax.axis_index("dp") * exp_dev
    hidden, shares = [], []
    for local in range(exp_dev):
        weights = jnp.concatenate([gate_ref[local], up_ref[local]])
        both = times_rows(rows_ref[:, :width], weights)
        gate, up = both[:, :units], both[:, units:]
        hidden.append((gate / (1.0 + jnp.exp(-gate)) * up).astype(jnp.bfloat16))
        mine = jnp.where(lane == first_expert + local, tags, 0.0)
        shares.append(jnp.sum(mine, axis=1, keepdims=True))
    block = min(512, width)

    @pl.loop(0, width // block)
    def _(index):
        columns = pl.ds(pl.multiple_of(index * block, block), block)
        total = 0.0
        for local in range(exp_dev):
            out = jnp.dot(
                hidden[local],
                down_ref[local, :, columns],
                preferred_element_type=jnp.float32,
            )
            total = total + out * shares[local]
        start = 0
        for result in results:
            stop = start + result.shape[0]
            result[:, columns] = total[start:stop].astype(result.dtype)
            start = stop


def run_experts(pieces, kinds, expert_total, w_gate, w_up, w_down):
    rows = sum(piece.shape[0] for piece in pieces)
    exp_dev, _, width = w_down.shape
    place = pltpu.VMEM if len(pieces) > 1 else jax.ShapeDtypeStruct
    return pl.pallas_call(
        functools.partial(expert_kernel, exp_dev, expert_total, len(pieces)),
        out_shape=[
            place((piece.shape[0], width), kind) for piece, kind in zip(pieces, kinds)
        ],
        in_specs=[IN_VMEM] * (len(pieces) + 3),
        out_specs=[IN_VMEM] * len(pieces),
        scratch_shapes=[pltpu.VMEM((rows, pieces[0].shape[1]), jnp.bfloat16)],
        compiler_params=pltpu.CompilerParams(vmem_limit_bytes=VMEM_BYTES),
        cost_estimate=pl.CostEstimate(
            flops=6 * rows * w_down.size, bytes_accessed=rows * width * 5, transcendentals=0
        ),
    )(*pieces, w_gate, w_up, w_down)


def body(tokens, expert_ids, router, w_gate, w_up, w_down):
    pieces = gather_rows(pack(tokens, expert_ids, router))
    kinds = [jnp.float32] * 2 + [jnp.bfloat16] * 2
    operands = (router.shape[0], w_gate, w_up, w_down)
    if sum(piece.shape[0] for piece in pieces) <= ROWS:
        results = run_experts(pieces, kinds, *operands)
    else:
        results = []
        for piece, kind in zip(pieces, kinds):
            chunks = [
                run_experts([piece[start : start + ROWS]], [kind], *operands)[0]
                for start in range(0, piece.shape[0], ROWS)
            ]
            results.append(cat(chunks))
    return scatter_sums(results[:2], results[2:])


def solution(mesh):
    in_specs = (
        P(("dp", "expert"), None),
        P(("dp", "expert"), None),
        P(),
        P("dp", "expert", None),
        P("dp", "expert", None),
        P("dp", "expert", None),
    )
    out_specs = P(("dp", "expert"), None)
    return jax.shard_map(body, mesh=mesh, in_specs=in_specs, out_specs=out_specs, check_vma=False)
```

```python
import functools

import jax
import jax.numpy as jnp
from jax import lax
from jax.experimental import pallas as pl
from jax.experimental.pallas import tpu as pltpu
from jax.sharding import PartitionSpec as P

LANES = 128
ROWS = 256
TERMS = 3
VMEM_BYTES = 24 * 1024 * 1024
SMALL_BYTES = 2 * 1024 * 1024
EXCHANGE_FLOPS = 20_000_000_000
IN_VMEM = pl.BlockSpec(memory_space=pltpu.VMEM)
ANYWHERE = pl.BlockSpec(memory_space=pl.ANY)


def times_rows(left, right):
    return lax.dot_general(
        left, right, (((1,), (1,)), ((), ())), preferred_element_type=jnp.float32
    )


def swap(value, axis, mask):
    count = lax.axis_size(axis)
    return lax.ppermute(value, axis, [(i, i ^ mask) for i in range(count)])


def send(value, step):
    return swap(value.astype(jnp.bfloat16), *step)


def wide(value):
    return value.astype(jnp.float32)


CORE = ("dp", 1)


def plane_steps():
    return [("dp", mask) for mask in range(lax.axis_size("dp") - 2, 0, -2)]


def cat(parts):
    return parts[0] if len(parts) == 1 else jnp.concatenate(parts)


def split(value, count):
    step = value.shape[0] // count
    return [value[start : start + step] for start in range(0, value.shape[0], step)]


def after(value, *others):
    return lax.optimization_barrier((value, *others))[0]


def gather_half(half, earlier):
    rest = [swap(half, *step) for step in plane_steps()]
    half = cat([half, after(rest[0], *earlier), *rest[1:]])
    return half, swap(half, *CORE)


def scatter_half(total):
    steps = plane_steps()
    part, *rest = split(total, len(steps) + 1)
    here = [send(other, step) for other, step in zip(rest, steps)]
    return sum([wide(other) for other in here], part)


def scatter_sums(early, late):
    count = lax.axis_size("expert") // 2
    total, *early = split(scatter_half(early), count)
    early = [send(part, ("expert", 2 * index + 2)) for index, part in enumerate(early)]
    total = sum([wide(part) for part in early], total)
    late = split(scatter_half(late), count)
    late = [send(part, ("expert", 2 * index + 1)) for index, part in enumerate(late)]
    return sum([wide(part) for part in late], total).astype(jnp.bfloat16)


def pack_kernel(tokens_hbm, ids_hbm, router_hbm, packed_ref, tokens_ref, ids_ref, router_ref, done):
    pairs = [(tokens_hbm, tokens_ref), (ids_hbm, ids_ref), (router_hbm, router_ref)]
    copies = [
        pltpu.make_async_copy(source, target, done.at[index])
        for index, (source, target) in enumerate(pairs)
    ]
    for copy in copies:
        copy.start()
    for copy in copies:
        copy.wait()
    tokens = tokens_ref[...]
    width, expert_total = tokens.shape[1], router_ref.shape[0]
    logits = times_rows(tokens, router_ref[...])
    experts = lax.broadcasted_iota(jnp.int32, logits.shape, 1)
    ids = ids_ref[...]
    chosen = experts < 0
    for pick in range(ids.shape[1]):
        chosen = jnp.logical_or(chosen, ids[:, pick : pick + 1] == experts)
    scores = jnp.where(chosen, 1.0 / (1.0 + jnp.exp(-logits)), 0.0)
    rest = scores / jnp.sum(scores, axis=1, keepdims=True)
    place = (expert_total, packed_ref.shape[1] - width)
    source, lane = [lax.broadcasted_iota(jnp.int32, place, axis) for axis in (0, 1)]
    tags = 0.0
    for term in range(TERMS):
        part = rest.astype(jnp.bfloat16)
        rest = rest - part.astype(jnp.float32)
        moved = (lane == source + term * expert_total).astype(jnp.float32).astype(jnp.bfloat16)
        tags = tags + jnp.dot(part, moved, preferred_element_type=jnp.float32)
    packed_ref[:, :width] = tokens
    packed_ref[:, width:] = tags.astype(jnp.bfloat16)


def pack(tokens, expert_ids, router):
    rows, width = tokens.shape
    extra = -(-TERMS * router.shape[0] // LANES) * LANES
    return pl.pallas_call(
        pack_kernel,
        out_shape=pltpu.VMEM((rows, width + extra), tokens.dtype),
        in_specs=[ANYWHERE] * 3,
        out_specs=IN_VMEM,
        scratch_shapes=[
            *[pltpu.VMEM(value.shape, value.dtype) for value in (tokens, expert_ids, router)],
            pltpu.SemaphoreType.DMA((3,)),
        ],
        compiler_params=pltpu.CompilerParams(vmem_limit_bytes=SMALL_BYTES),
        cost_estimate=pl.CostEstimate(
            flops=2 * rows * router.size, bytes_accessed=4 * router.size, transcendentals=0
        ),
    )(*[pltpu.with_memory_space_constraint(v, pltpu.HBM) for v in (tokens, expert_ids, router)])


def join_kernel(*refs):
    *parts, joined_ref = refs
    start = 0
    for part in parts:
        joined_ref[start : start + part.shape[0]] = part[...]
        start += part.shape[0]


def join(parts):
    rows, width = sum(part.shape[0] for part in parts), parts[0].shape[1]
    return pl.pallas_call(
        join_kernel,
        out_shape=pltpu.VMEM((rows, width), parts[0].dtype),
        in_specs=[IN_VMEM] * len(parts),
        out_specs=IN_VMEM,
        compiler_params=pltpu.CompilerParams(vmem_limit_bytes=SMALL_BYTES),
        cost_estimate=pl.CostEstimate(
            flops=EXCHANGE_FLOPS, bytes_accessed=0, transcendentals=0
        ),
    )(*parts)


def expert_kernel(exp_dev, expert_total, parts, *refs):
    pieces, refs = refs[:parts], refs[parts:]
    gate_ref, up_ref, down_ref, *results, rows_ref = refs
    units, width = down_ref.shape[1:]
    start = 0
    for piece in pieces:
        rows_ref[start : start + piece.shape[0]] = piece[...]
        start += piece.shape[0]
    tags = rows_ref[:, width:].astype(jnp.float32)
    lane = lax.rem(lax.broadcasted_iota(jnp.int32, tags.shape, 1), expert_total)
    first_expert = lax.axis_index("dp") * exp_dev
    hidden, shares = [], []
    for local in range(exp_dev):
        weights = jnp.concatenate([gate_ref[local], up_ref[local]])
        both = times_rows(rows_ref[:, :width], weights)
        gate, up = both[:, :units], both[:, units:]
        hidden.append((gate / (1.0 + jnp.exp(-gate)) * up).astype(jnp.bfloat16))
        mine = jnp.where(lane == first_expert + local, tags, 0.0)
        shares.append(jnp.sum(mine, axis=1, keepdims=True))
    block = min(512, width)

    @pl.loop(0, width // block)
    def _(index):
        columns = pl.ds(pl.multiple_of(index * block, block), block)
        total = 0.0
        for local in range(exp_dev):
            out = jnp.dot(
                hidden[local],
                down_ref[local, :, columns],
                preferred_element_type=jnp.float32,
            )
            total = total + out * shares[local]
        start = 0
        for result in results:
            stop = start + result.shape[0]
            result[:, columns] = total[start:stop].astype(result.dtype)
            start = stop


def run_experts(pieces, kinds, expert_total, w_gate, w_up, w_down):
    rows = sum(piece.shape[0] for piece in pieces)
    exp_dev, _, width = w_down.shape
    place = pltpu.VMEM if len(pieces) > 1 else jax.ShapeDtypeStruct
    return pl.pallas_call(
        functools.partial(expert_kernel, exp_dev, expert_total, len(pieces)),
        out_shape=[
            place((piece.shape[0], width), kind) for piece, kind in zip(pieces, kinds)
        ],
        in_specs=[IN_VMEM] * (len(pieces) + 3),
        out_specs=[IN_VMEM] * len(pieces),
        scratch_shapes=[pltpu.VMEM((rows, pieces[0].shape[1]), jnp.bfloat16)],
        compiler_params=pltpu.CompilerParams(vmem_limit_bytes=VMEM_BYTES),
        cost_estimate=pl.CostEstimate(
            flops=6 * rows * w_down.size, bytes_accessed=rows * width * 5, transcendentals=0
        ),
    )(*pieces, w_gate, w_up, w_down)


def half_experts(here, there, *operands):
    kinds = [jnp.float32, jnp.bfloat16]
    if 2 * here.shape[0] <= ROWS:
        return run_experts([here, there], kinds, *operands)
    results = []
    for piece, kind in zip((here, there), kinds):
        chunks = [
            run_experts([piece[start : start + ROWS]], [kind], *operands)[0]
            for start in range(0, piece.shape[0], ROWS)
        ]
        results.append(cat(chunks))
    return results


def body(tokens, expert_ids, router, w_gate, w_up, w_down):
    block = pack(tokens, expert_ids, router)
    column = [block] + [swap(block, "expert", mask) for mask in range(1, lax.axis_size("expert"))]
    operands = (router.shape[0], w_gate, w_up, w_down)
    half = cat(column[1::2])
    early = half_experts(*gather_half(join(column[0::2]), [half]), *operands)
    early_total = early[0] + wide(swap(early[1], *CORE))
    here, there = gather_half(half, early)
    late = half_experts(here, after(there, early_total), *operands)
    return scatter_sums(early_total, late[0] + wide(swap(late[1], *CORE)))


def solution(mesh):
    in_specs = (
        P(("dp", "expert"), None),
        P(("dp", "expert"), None),
        P(),
        P("dp", "expert", None),
        P("dp", "expert", None),
        P("dp", "expert", None),
    )
    out_specs = P(("dp", "expert"), None)
    return jax.shard_map(body, mesh=mesh, in_specs=in_specs, out_specs=out_specs, check_vma=False)
```

```python
import functools

import jax
import jax.numpy as jnp
from jax import lax
from jax.experimental import pallas as pl
from jax.experimental.pallas import tpu as pltpu
from jax.sharding import PartitionSpec as P

LANES = 128
ROWS = 256
TERMS = 3
VMEM_BYTES = 24 * 1024 * 1024
SMALL_BYTES = 2 * 1024 * 1024
EXCHANGE_FLOPS = 20_000_000_000
IN_VMEM = pl.BlockSpec(memory_space=pltpu.VMEM)
ANYWHERE = pl.BlockSpec(memory_space=pl.ANY)


def times_rows(left, right):
    return lax.dot_general(
        left, right, (((1,), (1,)), ((), ())), preferred_element_type=jnp.float32
    )


def swap(value, axis, mask):
    count = lax.axis_size(axis)
    return lax.ppermute(value, axis, [(i, i ^ mask) for i in range(count)])


def send(value, step):
    return swap(value.astype(jnp.bfloat16), *step)


def wide(value):
    return value.astype(jnp.float32)


CORE = ("dp", 1)


def plane_steps():
    return [("dp", mask) for mask in range(2, lax.axis_size("dp"), 2)]


def cat(parts):
    return parts[0] if len(parts) == 1 else jnp.concatenate(parts)


def split(value, count):
    step = value.shape[0] // count
    return [value[start : start + step] for start in range(0, value.shape[0], step)]


def after(value, *others):
    return lax.optimization_barrier((value, *others))[0]


def gather_rows(block):
    depth = lax.axis_size("expert")
    column = [block] + [swap(block, "expert", mask) for mask in range(1, depth)]
    near = join(column[: depth // 2])
    steps = plane_steps()
    near_rest = [swap(near, *step) for step in steps]
    far = cat(column[depth // 2 :])
    far_rest = [swap(far, *step) for step in steps]
    near = cat([near, *near_rest])
    near_there = swap(near, *CORE)
    far = cat([far, *far_rest])
    return [near, far, near_there, swap(far, *CORE)]


def scatter_sums(kept, away):
    steps, depth = plane_steps(), lax.axis_size("expert")
    sums, here = [], []
    for mine, other in reversed(list(zip(kept, away))):
        part, *rest = split(mine + wide(swap(other, *CORE)), len(steps) + 1)
        rest = [other.astype(jnp.bfloat16) for other in rest[::-1]]
        if here:
            rest = [after(other, here[0]) for other in rest]
        here = [send(other, step) for other, step in zip(rest, steps[::-1])]
        sums.append(sum([wide(other) for other in here], part))
    far, (total, *near) = split(sums[0], depth // 2), split(sums[1], depth // 2)
    far = [send(part, ("expert", mask + depth // 2)) for mask, part in enumerate(far)]
    near = [send(part, ("expert", mask + 1)) for mask, part in enumerate(near)]
    far = sum(wide(part) for part in far)
    far, *near = lax.optimization_barrier((far, *near))
    return sum([wide(part) for part in near], total + far).astype(jnp.bfloat16)


def pack_kernel(tokens_hbm, ids_hbm, router_hbm, packed_ref, tokens_ref, ids_ref, router_ref, done):
    pairs = [(tokens_hbm, tokens_ref), (ids_hbm, ids_ref), (router_hbm, router_ref)]
    copies = [
        pltpu.make_async_copy(source, target, done.at[index])
        for index, (source, target) in enumerate(pairs)
    ]
    for copy in copies:
        copy.start()
    for copy in copies:
        copy.wait()
    tokens = tokens_ref[...]
    width, expert_total = tokens.shape[1], router_ref.shape[0]
    logits = times_rows(tokens, router_ref[...])
    experts = lax.broadcasted_iota(jnp.int32, logits.shape, 1)
    ids = ids_ref[...]
    chosen = experts < 0
    for pick in range(ids.shape[1]):
        chosen = jnp.logical_or(chosen, ids[:, pick : pick + 1] == experts)
    scores = jnp.where(chosen, 1.0 / (1.0 + jnp.exp(-logits)), 0.0)
    rest = scores / jnp.sum(scores, axis=1, keepdims=True)
    place = (expert_total, packed_ref.shape[1] - width)
    source, lane = [lax.broadcasted_iota(jnp.int32, place, axis) for axis in (0, 1)]
    tags = 0.0
    for term in range(TERMS):
        part = rest.astype(jnp.bfloat16)
        rest = rest - part.astype(jnp.float32)
        moved = (lane == source + term * expert_total).astype(jnp.float32).astype(jnp.bfloat16)
        tags = tags + jnp.dot(part, moved, preferred_element_type=jnp.float32)
    packed_ref[:, :width] = tokens
    packed_ref[:, width:] = tags.astype(jnp.bfloat16)


def pack(tokens, expert_ids, router):
    rows, width = tokens.shape
    extra = -(-TERMS * router.shape[0] // LANES) * LANES
    return pl.pallas_call(
        pack_kernel,
        out_shape=pltpu.VMEM((rows, width + extra), tokens.dtype),
        in_specs=[ANYWHERE] * 3,
        out_specs=IN_VMEM,
        scratch_shapes=[
            *[pltpu.VMEM(value.shape, value.dtype) for value in (tokens, expert_ids, router)],
            pltpu.SemaphoreType.DMA((3,)),
        ],
        compiler_params=pltpu.CompilerParams(vmem_limit_bytes=SMALL_BYTES),
        cost_estimate=pl.CostEstimate(
            flops=2 * rows * router.size, bytes_accessed=4 * router.size, transcendentals=0
        ),
    )(*[pltpu.with_memory_space_constraint(v, pltpu.HBM) for v in (tokens, expert_ids, router)])


def join_kernel(*refs):
    *parts, joined_ref = refs
    start = 0
    for part in parts:
        joined_ref[start : start + part.shape[0]] = part[...]
        start += part.shape[0]


def join(parts):
    rows, width = sum(part.shape[0] for part in parts), parts[0].shape[1]
    return pl.pallas_call(
        join_kernel,
        out_shape=pltpu.VMEM((rows, width), parts[0].dtype),
        in_specs=[IN_VMEM] * len(parts),
        out_specs=IN_VMEM,
        compiler_params=pltpu.CompilerParams(vmem_limit_bytes=SMALL_BYTES),
        cost_estimate=pl.CostEstimate(
            flops=EXCHANGE_FLOPS, bytes_accessed=0, transcendentals=0
        ),
    )(*parts)


def expert_kernel(exp_dev, expert_total, parts, *refs):
    pieces, refs = refs[:parts], refs[parts:]
    gate_ref, up_ref, down_ref, *results, rows_ref = refs
    units, width = down_ref.shape[1:]
    start = 0
    for piece in pieces:
        rows_ref[start : start + piece.shape[0]] = piece[...]
        start += piece.shape[0]
    tags = rows_ref[:, width:].astype(jnp.float32)
    lane = lax.rem(lax.broadcasted_iota(jnp.int32, tags.shape, 1), expert_total)
    first_expert = lax.axis_index("dp") * exp_dev
    hidden, shares = [], []
    for local in range(exp_dev):
        weights = jnp.concatenate([gate_ref[local], up_ref[local]])
        both = times_rows(rows_ref[:, :width], weights)
        gate, up = both[:, :units], both[:, units:]
        hidden.append((gate / (1.0 + jnp.exp(-gate)) * up).astype(jnp.bfloat16))
        mine = jnp.where(lane == first_expert + local, tags, 0.0)
        shares.append(jnp.sum(mine, axis=1, keepdims=True))
    block = min(512, width)

    @pl.loop(0, width // block)
    def _(index):
        columns = pl.ds(pl.multiple_of(index * block, block), block)
        total = 0.0
        for local in range(exp_dev):
            out = jnp.dot(
                hidden[local],
                down_ref[local, :, columns],
                preferred_element_type=jnp.float32,
            )
            total = total + out * shares[local]
        start = 0
        for result in results:
            stop = start + result.shape[0]
            result[:, columns] = total[start:stop].astype(result.dtype)
            start = stop


def run_experts(pieces, kinds, expert_total, w_gate, w_up, w_down):
    rows = sum(piece.shape[0] for piece in pieces)
    exp_dev, _, width = w_down.shape
    place = pltpu.VMEM if len(pieces) > 1 else jax.ShapeDtypeStruct
    return pl.pallas_call(
        functools.partial(expert_kernel, exp_dev, expert_total, len(pieces)),
        out_shape=[
            place((piece.shape[0], width), kind) for piece, kind in zip(pieces, kinds)
        ],
        in_specs=[IN_VMEM] * (len(pieces) + 3),
        out_specs=[IN_VMEM] * len(pieces),
        scratch_shapes=[pltpu.VMEM((rows, pieces[0].shape[1]), jnp.bfloat16)],
        compiler_params=pltpu.CompilerParams(vmem_limit_bytes=VMEM_BYTES),
        cost_estimate=pl.CostEstimate(
            flops=6 * rows * w_down.size, bytes_accessed=rows * width * 5, transcendentals=0
        ),
    )(*pieces, w_gate, w_up, w_down)


def body(tokens, expert_ids, router, w_gate, w_up, w_down):
    pieces = gather_rows(pack(tokens, expert_ids, router))
    kinds = [jnp.float32] * 2 + [jnp.bfloat16] * 2
    operands = (router.shape[0], w_gate, w_up, w_down)
    if sum(piece.shape[0] for piece in pieces) <= ROWS:
        results = run_experts(pieces, kinds, *operands)
    else:
        results = []
        for piece, kind in zip(pieces, kinds):
            chunks = [
                run_experts([piece[start : start + ROWS]], [kind], *operands)[0]
                for start in range(0, piece.shape[0], ROWS)
            ]
            results.append(cat(chunks))
    return scatter_sums(results[:2], results[2:])


def solution(mesh):
    in_specs = (
        P(("dp", "expert"), None),
        P(("dp", "expert"), None),
        P(),
        P("dp", "expert", None),
        P("dp", "expert", None),
        P("dp", "expert", None),
    )
    out_specs = P(("dp", "expert"), None)
    return jax.shard_map(body, mesh=mesh, in_specs=in_specs, out_specs=out_specs, check_vma=False)
```

```python
import functools

import jax
import jax.numpy as jnp
from jax import lax
from jax.experimental import pallas as pl
from jax.experimental.pallas import tpu as pltpu
from jax.sharding import PartitionSpec as P

LANES = 128
ROWS = 256
TERMS = 3
VMEM_BYTES = 24 * 1024 * 1024
SMALL_BYTES = 2 * 1024 * 1024
EXCHANGE_FLOPS = 20_000_000_000
IN_VMEM = pl.BlockSpec(memory_space=pltpu.VMEM)
ANYWHERE = pl.BlockSpec(memory_space=pl.ANY)


def times_rows(left, right):
    return lax.dot_general(
        left, right, (((1,), (1,)), ((), ())), preferred_element_type=jnp.float32
    )


def swap(value, axis, mask):
    count = lax.axis_size(axis)
    return lax.ppermute(value, axis, [(i, i ^ mask) for i in range(count)])


def send(value, step):
    return swap(value.astype(jnp.bfloat16), *step)


def wide(value):
    return value.astype(jnp.float32)


CORE = ("dp", 1)


def plane_steps():
    return [("dp", mask) for mask in range(2, lax.axis_size("dp"), 2)]


def cat(parts):
    return parts[0] if len(parts) == 1 else jnp.concatenate(parts)


def split(value, count):
    step = value.shape[0] // count
    return [value[start : start + step] for start in range(0, value.shape[0], step)]


def after(value, *others):
    return lax.optimization_barrier((value, *others))[0]


def gather_near(near, steps):
    if len(steps) != 3:
        return [swap(near, *step) for step in steps]
    x, y, _ = steps
    near_x, near_y = swap(near, *x), swap(near, *y)
    over_y, over_x = swap(split(near_x, 2)[0], *y), swap(split(near_y, 2)[1], *x)
    return [near_x, near_y, over_y, over_x]


def gather_rows(block):
    depth = lax.axis_size("expert")
    column = [block] + [swap(block, "expert", mask) for mask in range(1, depth)]
    near = join(column[: depth // 2])
    steps = plane_steps()
    near_rest = gather_near(near, steps)
    far = cat([after(column[depth // 2], *near_rest[:2]), *column[depth // 2 + 1 :]])
    far_rest = [swap(far, *step) for step in steps]
    near = cat([near, *near_rest])
    near_there = swap(near, *CORE)
    far = cat([far, *far_rest])
    return [near, far, near_there, swap(far, *CORE)]


def scatter_sums(kept, away):
    steps, depth = plane_steps(), lax.axis_size("expert")
    near, far = [mine + wide(swap(other, *CORE)) for mine, other in zip(kept, away)]
    far, *rest = split(far, len(steps) + 1)
    far_here = [send(other, step) for other, step in zip(rest[::-1], steps[::-1])]
    far = sum([wide(other) for other in far_here], far)
    near, *rest = split(near, len(steps) + 1)
    if len(steps) == 3:
        x, y, _ = steps
        (x_first, x_last), (y_first, y_last), (over_y, over_x) = [split(part, 2) for part in rest]
        x_first = x_first + wide(send(over_y, y))
        y_last = y_last + wide(send(over_x, x))
        rest, steps = [cat([x_first, x_last]), cat([y_first, y_last])], [x, y]
    rest = [after(other.astype(jnp.bfloat16), far_here[0]) for other in rest[::-1]]
    near_here = [send(other, step) for other, step in zip(rest, steps[::-1])]
    sums = [far, sum([wide(other) for other in near_here], near)]
    far, (total, *near) = split(sums[0], depth // 2), split(sums[1], depth // 2)
    far = [send(part, ("expert", mask + depth // 2)) for mask, part in enumerate(far)]
    near = [send(part, ("expert", mask + 1)) for mask, part in enumerate(near)]
    far = sum(wide(part) for part in far)
    far, *near = lax.optimization_barrier((far, *near))
    return sum([wide(part) for part in near], total + far).astype(jnp.bfloat16)


def pack_kernel(tokens_hbm, ids_hbm, router_hbm, packed_ref, tokens_ref, ids_ref, router_ref, done):
    pairs = [(tokens_hbm, tokens_ref), (ids_hbm, ids_ref), (router_hbm, router_ref)]
    copies = [
        pltpu.make_async_copy(source, target, done.at[index])
        for index, (source, target) in enumerate(pairs)
    ]
    for copy in copies:
        copy.start()
    for copy in copies:
        copy.wait()
    tokens = tokens_ref[...]
    width, expert_total = tokens.shape[1], router_ref.shape[0]
    logits = times_rows(tokens, router_ref[...])
    experts = lax.broadcasted_iota(jnp.int32, logits.shape, 1)
    ids = ids_ref[...]
    chosen = experts < 0
    for pick in range(ids.shape[1]):
        chosen = jnp.logical_or(chosen, ids[:, pick : pick + 1] == experts)
    scores = jnp.where(chosen, 1.0 / (1.0 + jnp.exp(-logits)), 0.0)
    rest = scores / jnp.sum(scores, axis=1, keepdims=True)
    place = (expert_total, packed_ref.shape[1] - width)
    source, lane = [lax.broadcasted_iota(jnp.int32, place, axis) for axis in (0, 1)]
    tags = 0.0
    for term in range(TERMS):
        part = rest.astype(jnp.bfloat16)
        rest = rest - part.astype(jnp.float32)
        moved = (lane == source + term * expert_total).astype(jnp.float32).astype(jnp.bfloat16)
        tags = tags + jnp.dot(part, moved, preferred_element_type=jnp.float32)
    packed_ref[:, :width] = tokens
    packed_ref[:, width:] = tags.astype(jnp.bfloat16)


def pack(tokens, expert_ids, router):
    rows, width = tokens.shape
    extra = -(-TERMS * router.shape[0] // LANES) * LANES
    return pl.pallas_call(
        pack_kernel,
        out_shape=pltpu.VMEM((rows, width + extra), tokens.dtype),
        in_specs=[ANYWHERE] * 3,
        out_specs=IN_VMEM,
        scratch_shapes=[
            *[pltpu.VMEM(value.shape, value.dtype) for value in (tokens, expert_ids, router)],
            pltpu.SemaphoreType.DMA((3,)),
        ],
        compiler_params=pltpu.CompilerParams(vmem_limit_bytes=SMALL_BYTES),
        cost_estimate=pl.CostEstimate(
            flops=2 * rows * router.size, bytes_accessed=4 * router.size, transcendentals=0
        ),
    )(*[pltpu.with_memory_space_constraint(v, pltpu.HBM) for v in (tokens, expert_ids, router)])


def join_kernel(*refs):
    *parts, joined_ref = refs
    start = 0
    for part in parts:
        joined_ref[start : start + part.shape[0]] = part[...]
        start += part.shape[0]


def join(parts):
    rows, width = sum(part.shape[0] for part in parts), parts[0].shape[1]
    return pl.pallas_call(
        join_kernel,
        out_shape=pltpu.VMEM((rows, width), parts[0].dtype),
        in_specs=[IN_VMEM] * len(parts),
        out_specs=IN_VMEM,
        compiler_params=pltpu.CompilerParams(vmem_limit_bytes=SMALL_BYTES),
        cost_estimate=pl.CostEstimate(
            flops=EXCHANGE_FLOPS, bytes_accessed=0, transcendentals=0
        ),
    )(*parts)


def expert_kernel(exp_dev, expert_total, parts, *refs):
    pieces, refs = refs[:parts], refs[parts:]
    gate_ref, up_ref, down_ref, *results, rows_ref = refs
    units, width = down_ref.shape[1:]
    start = 0
    for piece in pieces:
        rows_ref[start : start + piece.shape[0]] = piece[...]
        start += piece.shape[0]
    tags = rows_ref[:, width:].astype(jnp.float32)
    lane = lax.rem(lax.broadcasted_iota(jnp.int32, tags.shape, 1), expert_total)
    first_expert = lax.axis_index("dp") * exp_dev
    hidden, shares = [], []
    for local in range(exp_dev):
        weights = jnp.concatenate([gate_ref[local], up_ref[local]])
        both = times_rows(rows_ref[:, :width], weights)
        gate, up = both[:, :units], both[:, units:]
        hidden.append((gate / (1.0 + jnp.exp(-gate)) * up).astype(jnp.bfloat16))
        mine = jnp.where(lane == first_expert + local, tags, 0.0)
        shares.append(jnp.sum(mine, axis=1, keepdims=True))
    block = min(512, width)

    @pl.loop(0, width // block)
    def _(index):
        columns = pl.ds(pl.multiple_of(index * block, block), block)
        total = 0.0
        for local in range(exp_dev):
            out = jnp.dot(
                hidden[local],
                down_ref[local, :, columns],
                preferred_element_type=jnp.float32,
            )
            total = total + out * shares[local]
        start = 0
        for result in results:
            stop = start + result.shape[0]
            result[:, columns] = total[start:stop].astype(result.dtype)
            start = stop


def run_experts(pieces, kinds, expert_total, w_gate, w_up, w_down):
    rows = sum(piece.shape[0] for piece in pieces)
    exp_dev, _, width = w_down.shape
    place = pltpu.VMEM if len(pieces) > 1 else jax.ShapeDtypeStruct
    return pl.pallas_call(
        functools.partial(expert_kernel, exp_dev, expert_total, len(pieces)),
        out_shape=[
            place((piece.shape[0], width), kind) for piece, kind in zip(pieces, kinds)
        ],
        in_specs=[IN_VMEM] * (len(pieces) + 3),
        out_specs=[IN_VMEM] * len(pieces),
        scratch_shapes=[pltpu.VMEM((rows, pieces[0].shape[1]), jnp.bfloat16)],
        compiler_params=pltpu.CompilerParams(vmem_limit_bytes=VMEM_BYTES),
        cost_estimate=pl.CostEstimate(
            flops=6 * rows * w_down.size, bytes_accessed=rows * width * 5, transcendentals=0
        ),
    )(*pieces, w_gate, w_up, w_down)


def body(tokens, expert_ids, router, w_gate, w_up, w_down):
    pieces = gather_rows(pack(tokens, expert_ids, router))
    kinds = [jnp.float32] * 2 + [jnp.bfloat16] * 2
    operands = (router.shape[0], w_gate, w_up, w_down)
    if sum(piece.shape[0] for piece in pieces) <= ROWS:
        results = run_experts(pieces, kinds, *operands)
    else:
        results = []
        for piece, kind in zip(pieces, kinds):
            chunks = [
                run_experts([piece[start : start + ROWS]], [kind], *operands)[0]
                for start in range(0, piece.shape[0], ROWS)
            ]
            results.append(cat(chunks))
    return scatter_sums(results[:2], results[2:])


def solution(mesh):
    in_specs = (
        P(("dp", "expert"), None),
        P(("dp", "expert"), None),
        P(),
        P("dp", "expert", None),
        P("dp", "expert", None),
        P("dp", "expert", None),
    )
    out_specs = P(("dp", "expert"), None)
    return jax.shard_map(body, mesh=mesh, in_specs=in_specs, out_specs=out_specs, check_vma=False)
```

```python
import functools

import jax
import jax.numpy as jnp
from jax import lax
from jax.experimental import pallas as pl
from jax.experimental.pallas import tpu as pltpu
from jax.sharding import PartitionSpec as P

LANES = 128
ROWS = 256
TERMS = 3
VMEM_BYTES = 24 * 1024 * 1024
SMALL_BYTES = 2 * 1024 * 1024
EXCHANGE_FLOPS = 20_000_000_000
IN_VMEM = pl.BlockSpec(memory_space=pltpu.VMEM)
ANYWHERE = pl.BlockSpec(memory_space=pl.ANY)


def times_rows(left, right):
    return lax.dot_general(
        left, right, (((1,), (1,)), ((), ())), preferred_element_type=jnp.float32
    )


def swap(value, axis, mask):
    count = lax.axis_size(axis)
    return lax.ppermute(value, axis, [(i, i ^ mask) for i in range(count)])


def send(value, step):
    return swap(value.astype(jnp.bfloat16), *step)


def wide(value):
    return value.astype(jnp.float32)


CORE = ("dp", 1)


def plane_steps():
    return [("dp", mask) for mask in range(2, lax.axis_size("dp"), 2)]


def cat(parts):
    return parts[0] if len(parts) == 1 else jnp.concatenate(parts)


def split(value, count):
    step = value.shape[0] // count
    return [value[start : start + step] for start in range(0, value.shape[0], step)]


def after(value, *others):
    return lax.optimization_barrier((value, *others))[0]


def gather_rows(block):
    depth = lax.axis_size("expert")
    column = [block] + [swap(block, "expert", mask) for mask in range(1, depth)]
    near = join(column[: depth // 2])
    steps = plane_steps()
    near_rest = [swap(near, *step) for step in steps]
    far = cat(column[depth // 2 :])
    far_rest = [swap(far, *step) for step in steps]
    near = cat([near, *near_rest])
    near_there = swap(near, *CORE)
    far = cat([far, *far_rest])
    return [near, far, near_there, swap(far, *CORE)]


def scatter_sums(kept, away):
    steps, depth = plane_steps(), lax.axis_size("expert")
    sums, here = [], []
    for mine, other in reversed(list(zip(kept, away))):
        part, *rest = split(mine + wide(swap(other, *CORE)), len(steps) + 1)
        rest = [other.astype(jnp.bfloat16) for other in rest[::-1]]
        if here:
            rest = [after(other, here[0]) for other in rest]
        here = [send(other, step) for other, step in zip(rest, steps[::-1])]
        sums.append(sum([wide(other) for other in here], part))
    far, (total, *near) = split(sums[0], depth // 2), split(sums[1], depth // 2)
    far = [send(part, ("expert", mask + depth // 2)) for mask, part in enumerate(far)]
    near = [send(part, ("expert", mask + 1)) for mask, part in enumerate(near)]
    far = sum(wide(part) for part in far)
    far, *near = lax.optimization_barrier((far, *near))
    return sum([wide(part) for part in near], total + far).astype(jnp.bfloat16)


def pack_kernel(tokens_hbm, ids_hbm, router_hbm, packed_ref, tokens_ref, ids_ref, router_ref, done):
    pairs = [(tokens_hbm, tokens_ref), (ids_hbm, ids_ref), (router_hbm, router_ref)]
    copies = [
        pltpu.make_async_copy(source, target, done.at[index])
        for index, (source, target) in enumerate(pairs)
    ]
    for copy in copies:
        copy.start()
    for copy in copies:
        copy.wait()
    tokens = tokens_ref[...]
    width, expert_total = tokens.shape[1], router_ref.shape[0]
    logits = times_rows(tokens, router_ref[...])
    experts = lax.broadcasted_iota(jnp.int32, logits.shape, 1)
    ids = ids_ref[...]
    chosen = experts < 0
    for pick in range(ids.shape[1]):
        chosen = jnp.logical_or(chosen, ids[:, pick : pick + 1] == experts)
    scores = jnp.where(chosen, 1.0 / (1.0 + jnp.exp(-logits)), 0.0)
    rest = scores / jnp.sum(scores, axis=1, keepdims=True)
    place = (expert_total, packed_ref.shape[1] - width)
    source, lane = [lax.broadcasted_iota(jnp.int32, place, axis) for axis in (0, 1)]
    tags = 0.0
    for term in range(TERMS):
        part = rest.astype(jnp.bfloat16)
        rest = rest - part.astype(jnp.float32)
        moved = (lane == source + term * expert_total).astype(jnp.float32).astype(jnp.bfloat16)
        tags = tags + jnp.dot(part, moved, preferred_element_type=jnp.float32)
    packed_ref[:, :width] = tokens
    packed_ref[:, width:] = tags.astype(jnp.bfloat16)


def pack(tokens, expert_ids, router):
    rows, width = tokens.shape
    extra = -(-TERMS * router.shape[0] // LANES) * LANES
    return pl.pallas_call(
        pack_kernel,
        out_shape=pltpu.VMEM((rows, width + extra), tokens.dtype),
        in_specs=[ANYWHERE] * 3,
        out_specs=IN_VMEM,
        scratch_shapes=[
            *[pltpu.VMEM(value.shape, value.dtype) for value in (tokens, expert_ids, router)],
            pltpu.SemaphoreType.DMA((3,)),
        ],
        compiler_params=pltpu.CompilerParams(vmem_limit_bytes=SMALL_BYTES),
        cost_estimate=pl.CostEstimate(
            flops=2 * rows * router.size, bytes_accessed=4 * router.size, transcendentals=0
        ),
    )(*[pltpu.with_memory_space_constraint(v, pltpu.HBM) for v in (tokens, expert_ids, router)])


def join_kernel(*refs):
    *parts, joined_ref = refs
    start = 0
    for part in parts:
        joined_ref[start : start + part.shape[0]] = part[...]
        start += part.shape[0]


def join(parts):
    rows, width = sum(part.shape[0] for part in parts), parts[0].shape[1]
    return pl.pallas_call(
        join_kernel,
        out_shape=pltpu.VMEM((rows, width), parts[0].dtype),
        in_specs=[IN_VMEM] * len(parts),
        out_specs=IN_VMEM,
        compiler_params=pltpu.CompilerParams(vmem_limit_bytes=SMALL_BYTES),
        cost_estimate=pl.CostEstimate(
            flops=EXCHANGE_FLOPS, bytes_accessed=0, transcendentals=0
        ),
    )(*parts)


def expert_kernel(exp_dev, expert_total, parts, *refs):
    pieces, refs = refs[:parts], refs[parts:]
    gate_ref, up_ref, down_ref, *results, rows_ref = refs
    units, width = down_ref.shape[1:]
    start = 0
    for piece in pieces:
        rows_ref[start : start + piece.shape[0]] = piece[...]
        start += piece.shape[0]
    tags = rows_ref[:, width:].astype(jnp.float32)
    lane = lax.rem(lax.broadcasted_iota(jnp.int32, tags.shape, 1), expert_total)
    first_expert = lax.axis_index("dp") * exp_dev
    hidden, shares = [], []
    for local in range(exp_dev):
        weights = jnp.concatenate([gate_ref[local], up_ref[local]])
        both = times_rows(rows_ref[:, :width], weights)
        gate, up = both[:, :units], both[:, units:]
        hidden.append((gate / (1.0 + jnp.exp(-gate)) * up).astype(jnp.bfloat16))
        mine = jnp.where(lane == first_expert + local, tags, 0.0)
        shares.append(jnp.sum(mine, axis=1, keepdims=True))
    block = min(1024, width)
    for first in range(0, width, block):
        total = 0.0
        for local in range(exp_dev):
            out = jnp.dot(
                hidden[local],
                down_ref[local, :, first : first + block],
                preferred_element_type=jnp.float32,
            )
            total = total + out * shares[local]
        start = 0
        for result in results:
            stop = start + result.shape[0]
            result[:, first : first + block] = total[start:stop].astype(result.dtype)
            start = stop


def run_experts(pieces, kinds, expert_total, w_gate, w_up, w_down):
    rows = sum(piece.shape[0] for piece in pieces)
    exp_dev, _, width = w_down.shape
    place = pltpu.VMEM if len(pieces) > 1 else jax.ShapeDtypeStruct
    return pl.pallas_call(
        functools.partial(expert_kernel, exp_dev, expert_total, len(pieces)),
        out_shape=[
            place((piece.shape[0], width), kind) for piece, kind in zip(pieces, kinds)
        ],
        in_specs=[IN_VMEM] * (len(pieces) + 3),
        out_specs=[IN_VMEM] * len(pieces),
        scratch_shapes=[pltpu.VMEM((rows, pieces[0].shape[1]), jnp.bfloat16)],
        compiler_params=pltpu.CompilerParams(vmem_limit_bytes=VMEM_BYTES),
        cost_estimate=pl.CostEstimate(
            flops=6 * rows * w_down.size, bytes_accessed=rows * width * 5, transcendentals=0
        ),
    )(*pieces, w_gate, w_up, w_down)


def body(tokens, expert_ids, router, w_gate, w_up, w_down):
    pieces = gather_rows(pack(tokens, expert_ids, router))
    kinds = [jnp.float32] * 2 + [jnp.bfloat16] * 2
    operands = (router.shape[0], w_gate, w_up, w_down)
    if sum(piece.shape[0] for piece in pieces) <= ROWS:
        results = run_experts(pieces, kinds, *operands)
    else:
        results = []
        for piece, kind in zip(pieces, kinds):
            chunks = [
                run_experts([piece[start : start + ROWS]], [kind], *operands)[0]
                for start in range(0, piece.shape[0], ROWS)
            ]
            results.append(cat(chunks))
    return scatter_sums(results[:2], results[2:])


def solution(mesh):
    in_specs = (
        P(("dp", "expert"), None),
        P(("dp", "expert"), None),
        P(),
        P("dp", "expert", None),
        P("dp", "expert", None),
        P("dp", "expert", None),
    )
    out_specs = P(("dp", "expert"), None)
    return jax.shard_map(body, mesh=mesh, in_specs=in_specs, out_specs=out_specs, check_vma=False)
```

```python
import functools

import jax
import jax.numpy as jnp
from jax import lax
from jax.experimental import pallas as pl
from jax.experimental.pallas import tpu as pltpu
from jax.sharding import PartitionSpec as P

LANES = 128
ROWS = 256
TERMS = 3
VMEM_BYTES = 24 * 1024 * 1024
SMALL_BYTES = 2 * 1024 * 1024
EXCHANGE_FLOPS = 20_000_000_000
IN_VMEM = pl.BlockSpec(memory_space=pltpu.VMEM)
ANYWHERE = pl.BlockSpec(memory_space=pl.ANY)


def times_rows(left, right):
    return lax.dot_general(
        left, right, (((1,), (1,)), ((), ())), preferred_element_type=jnp.float32
    )


def swap(value, axis, mask):
    count = lax.axis_size(axis)
    return lax.ppermute(value, axis, [(i, i ^ mask) for i in range(count)])


def send(value, step):
    return swap(value.astype(jnp.bfloat16), *step)


def wide(value):
    return value.astype(jnp.float32)


CORE = ("dp", 1)


def plane_steps():
    return [("dp", mask) for mask in range(2, lax.axis_size("dp"), 2)]


def cat(parts):
    return parts[0] if len(parts) == 1 else jnp.concatenate(parts)


def split(value, count):
    step = value.shape[0] // count
    return [value[start : start + step] for start in range(0, value.shape[0], step)]


def after(value, *others):
    return lax.optimization_barrier((value, *others))[0]


def gather_rows(block):
    depth = lax.axis_size("expert")
    column = [block] + [swap(block, "expert", mask) for mask in range(1, depth)]
    near = join(column[: depth // 2])
    steps = plane_steps()
    near_rest = [swap(near, *step) for step in steps]
    far = cat(column[depth // 2 :])
    far_rest = [swap(far, *step) for step in steps]
    near = cat([near, *near_rest])
    near_there = swap(near, *CORE)
    far = cat([far, *far_rest])
    return [near, far, near_there, swap(far, *CORE)]


def scatter_sums(kept, away):
    steps, depth = plane_steps(), lax.axis_size("expert")
    sums, here = [], []
    for mine, other in reversed(list(zip(kept, away))):
        part, *rest = split(mine + wide(swap(other, *CORE)), len(steps) + 1)
        rest = [other.astype(jnp.bfloat16) for other in rest[::-1]]
        if here:
            rest = [after(other, here[0]) for other in rest]
        here = [send(other, step) for other, step in zip(rest, steps[::-1])]
        sums.append(sum([wide(other) for other in here], part))
    far, (total, *near) = split(sums[0], depth // 2), split(sums[1], depth // 2)
    far = [send(part, ("expert", mask + depth // 2)) for mask, part in enumerate(far)]
    near = [send(part, ("expert", mask + 1)) for mask, part in enumerate(near)]
    far = sum(wide(part) for part in far)
    far, *near = lax.optimization_barrier((far, *near))
    return sum([wide(part) for part in near], total + far).astype(jnp.bfloat16)


def pack_kernel(tokens_hbm, ids_hbm, router_hbm, packed_ref, tokens_ref, ids_ref, router_ref, done):
    pairs = [(tokens_hbm, tokens_ref), (ids_hbm, ids_ref), (router_hbm, router_ref)]
    copies = [
        pltpu.make_async_copy(source, target, done.at[index])
        for index, (source, target) in enumerate(pairs)
    ]
    for copy in copies:
        copy.start()
    for copy in copies:
        copy.wait()
    tokens = tokens_ref[...]
    width, expert_total = tokens.shape[1], router_ref.shape[0]
    logits = times_rows(tokens, router_ref[...])
    experts = lax.broadcasted_iota(jnp.int32, logits.shape, 1)
    ids = ids_ref[...]
    chosen = experts < 0
    for pick in range(ids.shape[1]):
        chosen = jnp.logical_or(chosen, ids[:, pick : pick + 1] == experts)
    scores = jnp.where(chosen, 1.0 / (1.0 + jnp.exp(-logits)), 0.0)
    rest = scores / jnp.sum(scores, axis=1, keepdims=True)
    place = (expert_total, packed_ref.shape[1] - width)
    source, lane = [lax.broadcasted_iota(jnp.int32, place, axis) for axis in (0, 1)]
    tags = 0.0
    for term in range(TERMS):
        part = rest.astype(jnp.bfloat16)
        rest = rest - part.astype(jnp.float32)
        moved = (lane == source + term * expert_total).astype(jnp.float32).astype(jnp.bfloat16)
        tags = tags + jnp.dot(part, moved, preferred_element_type=jnp.float32)
    packed_ref[:, :width] = tokens
    packed_ref[:, width:] = tags.astype(jnp.bfloat16)


def pack(tokens, expert_ids, router):
    rows, width = tokens.shape
    extra = -(-TERMS * router.shape[0] // LANES) * LANES
    return pl.pallas_call(
        pack_kernel,
        out_shape=pltpu.VMEM((rows, width + extra), tokens.dtype),
        in_specs=[ANYWHERE] * 3,
        out_specs=IN_VMEM,
        scratch_shapes=[
            *[pltpu.VMEM(value.shape, value.dtype) for value in (tokens, expert_ids, router)],
            pltpu.SemaphoreType.DMA((3,)),
        ],
        compiler_params=pltpu.CompilerParams(vmem_limit_bytes=SMALL_BYTES),
        cost_estimate=pl.CostEstimate(
            flops=2 * rows * router.size, bytes_accessed=4 * router.size, transcendentals=0
        ),
    )(*[pltpu.with_memory_space_constraint(v, pltpu.HBM) for v in (tokens, expert_ids, router)])


def join_kernel(*refs):
    *parts, joined_ref = refs
    start = 0
    for part in parts:
        joined_ref[start : start + part.shape[0]] = part[...]
        start += part.shape[0]


def join(parts):
    rows, width = sum(part.shape[0] for part in parts), parts[0].shape[1]
    return pl.pallas_call(
        join_kernel,
        out_shape=pltpu.VMEM((rows, width), parts[0].dtype),
        in_specs=[IN_VMEM] * len(parts),
        out_specs=IN_VMEM,
        compiler_params=pltpu.CompilerParams(vmem_limit_bytes=SMALL_BYTES),
        cost_estimate=pl.CostEstimate(
            flops=EXCHANGE_FLOPS, bytes_accessed=0, transcendentals=0
        ),
    )(*parts)


def expert_kernel(exp_dev, expert_total, parts, *refs):
    pieces, refs = refs[:parts], refs[parts:]
    gate_ref, up_ref, down_ref, *results = refs
    units, width = down_ref.shape[1:]
    rows = jnp.concatenate([piece[...] for piece in pieces])
    tags = rows[:, width:].astype(jnp.float32)
    lane = lax.rem(lax.broadcasted_iota(jnp.int32, tags.shape, 1), expert_total)
    first_expert = lax.axis_index("dp") * exp_dev
    weights = [ref[local] for local in range(exp_dev) for ref in (gate_ref, up_ref)]
    both = times_rows(rows[:, :width], jnp.concatenate(weights))
    hidden, shares = [], []
    for local in range(exp_dev):
        middle = (2 * local + 1) * units
        gate, up = both[:, middle - units : middle], both[:, middle : middle + units]
        hidden.append((gate / (1.0 + jnp.exp(-gate)) * up).astype(jnp.bfloat16))
        mine = jnp.where(lane == first_expert + local, tags, 0.0)
        shares.append(jnp.sum(mine, axis=1, keepdims=True))
    block = min(2048, width)
    for first in range(0, width, block):
        total = 0.0
        for local in range(exp_dev):
            out = jnp.dot(
                hidden[local],
                down_ref[local, :, first : first + block],
                preferred_element_type=jnp.float32,
            )
            total = total + out * shares[local]
        start = 0
        for result in results:
            stop = start + result.shape[0]
            result[:, first : first + block] = total[start:stop].astype(result.dtype)
            start = stop


def run_experts(pieces, kinds, expert_total, w_gate, w_up, w_down):
    rows = sum(piece.shape[0] for piece in pieces)
    exp_dev, _, width = w_down.shape
    place = pltpu.VMEM if len(pieces) > 1 else jax.ShapeDtypeStruct
    return pl.pallas_call(
        functools.partial(expert_kernel, exp_dev, expert_total, len(pieces)),
        out_shape=[
            place((piece.shape[0], width), kind) for piece, kind in zip(pieces, kinds)
        ],
        in_specs=[IN_VMEM] * (len(pieces) + 3),
        out_specs=[IN_VMEM] * len(pieces),
        compiler_params=pltpu.CompilerParams(vmem_limit_bytes=VMEM_BYTES),
        cost_estimate=pl.CostEstimate(
            flops=6 * rows * w_down.size, bytes_accessed=rows * width * 5, transcendentals=0
        ),
    )(*pieces, w_gate, w_up, w_down)


def body(tokens, expert_ids, router, w_gate, w_up, w_down):
    pieces = gather_rows(pack(tokens, expert_ids, router))
    kinds = [jnp.float32] * 2 + [jnp.bfloat16] * 2
    operands = (router.shape[0], w_gate, w_up, w_down)
    if sum(piece.shape[0] for piece in pieces) <= ROWS:
        results = run_experts(pieces, kinds, *operands)
    else:
        results = []
        for piece, kind in zip(pieces, kinds):
            chunks = [
                run_experts([piece[start : start + ROWS]], [kind], *operands)[0]
                for start in range(0, piece.shape[0], ROWS)
            ]
            results.append(cat(chunks))
    return scatter_sums(results[:2], results[2:])


def solution(mesh):
    in_specs = (
        P(("dp", "expert"), None),
        P(("dp", "expert"), None),
        P(),
        P("dp", "expert", None),
        P("dp", "expert", None),
        P("dp", "expert", None),
    )
    out_specs = P(("dp", "expert"), None)
    return jax.shard_map(body, mesh=mesh, in_specs=in_specs, out_specs=out_specs, check_vma=False)
```

```python
import functools

import jax
import jax.numpy as jnp
from jax import lax
from jax.experimental import pallas as pl
from jax.experimental.pallas import tpu as pltpu
from jax.sharding import PartitionSpec as P

LANES = 128
ROWS = 256
TERMS = 3
VMEM_BYTES = 24 * 1024 * 1024
SMALL_BYTES = 2 * 1024 * 1024
EXCHANGE_FLOPS = 20_000_000_000
IN_VMEM = pl.BlockSpec(memory_space=pltpu.VMEM)
ANYWHERE = pl.BlockSpec(memory_space=pl.ANY)


def times_rows(left, right):
    return lax.dot_general(
        left, right, (((1,), (1,)), ((), ())), preferred_element_type=jnp.float32
    )


def swap(value, axis, mask):
    count = lax.axis_size(axis)
    return lax.ppermute(value, axis, [(i, i ^ mask) for i in range(count)])


def send(value, step):
    return swap(value.astype(jnp.bfloat16), *step)


def wide(value):
    return value.astype(jnp.float32)


CORE = ("dp", 1)


def plane_steps():
    return [("dp", mask) for mask in range(2, lax.axis_size("dp"), 2)]


def cat(parts):
    return parts[0] if len(parts) == 1 else jnp.concatenate(parts)


def split(value, count):
    step = value.shape[0] // count
    return [value[start : start + step] for start in range(0, value.shape[0], step)]


def after(value, *others):
    return lax.optimization_barrier((value, *others))[0]


def gather_rows(block):
    depth = lax.axis_size("expert")
    column = [block] + [swap(block, "expert", mask) for mask in range(1, depth)]
    near = join(column[: depth // 2])
    steps = plane_steps()
    near_rest = [swap(near, *step) for step in steps]
    far = cat(column[depth // 2 :])
    far_rest = [swap(far, *step) for step in steps]
    near = cat([near, *near_rest])
    near_there = swap(near, *CORE)
    far = cat([far, *far_rest])
    return [near, far, near_there, swap(far, *CORE)]


def scatter_sums(kept, away):
    steps, depth = plane_steps(), lax.axis_size("expert")
    sums, here = [], []
    for mine, other in reversed(list(zip(kept, away))):
        part, *rest = split(mine + wide(swap(other, *CORE)), len(steps) + 1)
        rest = [other.astype(jnp.bfloat16) for other in rest[::-1]]
        if here:
            rest = rest[:1] + [after(other, here[0]) for other in rest[1:]]
        here = [send(other, step) for other, step in zip(rest, steps[::-1])]
        sums.append(sum([wide(other) for other in here], part))
    far, (total, *near) = split(sums[0], depth // 2), split(sums[1], depth // 2)
    far = [send(part, ("expert", mask + depth // 2)) for mask, part in enumerate(far)]
    near = [send(part, ("expert", mask + 1)) for mask, part in enumerate(near)]
    far = sum(wide(part) for part in far)
    far, *near = lax.optimization_barrier((far, *near))
    return sum([wide(part) for part in near], total + far).astype(jnp.bfloat16)


def pack_kernel(tokens_hbm, ids_hbm, router_hbm, packed_ref, tokens_ref, ids_ref, router_ref, done):
    pairs = [(tokens_hbm, tokens_ref), (ids_hbm, ids_ref), (router_hbm, router_ref)]
    copies = [
        pltpu.make_async_copy(source, target, done.at[index])
        for index, (source, target) in enumerate(pairs)
    ]
    for copy in copies:
        copy.start()
    for copy in copies:
        copy.wait()
    tokens = tokens_ref[...]
    width, expert_total = tokens.shape[1], router_ref.shape[0]
    logits = times_rows(tokens, router_ref[...])
    experts = lax.broadcasted_iota(jnp.int32, logits.shape, 1)
    ids = ids_ref[...]
    chosen = experts < 0
    for pick in range(ids.shape[1]):
        chosen = jnp.logical_or(chosen, ids[:, pick : pick + 1] == experts)
    scores = jnp.where(chosen, 1.0 / (1.0 + jnp.exp(-logits)), 0.0)
    rest = scores / jnp.sum(scores, axis=1, keepdims=True)
    place = (expert_total, packed_ref.shape[1] - width)
    source, lane = [lax.broadcasted_iota(jnp.int32, place, axis) for axis in (0, 1)]
    tags = 0.0
    for term in range(TERMS):
        part = rest.astype(jnp.bfloat16)
        rest = rest - part.astype(jnp.float32)
        moved = (lane == source + term * expert_total).astype(jnp.float32).astype(jnp.bfloat16)
        tags = tags + jnp.dot(part, moved, preferred_element_type=jnp.float32)
    packed_ref[:, :width] = tokens
    packed_ref[:, width:] = tags.astype(jnp.bfloat16)


def pack(tokens, expert_ids, router):
    rows, width = tokens.shape
    extra = -(-TERMS * router.shape[0] // LANES) * LANES
    return pl.pallas_call(
        pack_kernel,
        out_shape=pltpu.VMEM((rows, width + extra), tokens.dtype),
        in_specs=[ANYWHERE] * 3,
        out_specs=IN_VMEM,
        scratch_shapes=[
            *[pltpu.VMEM(value.shape, value.dtype) for value in (tokens, expert_ids, router)],
            pltpu.SemaphoreType.DMA((3,)),
        ],
        compiler_params=pltpu.CompilerParams(vmem_limit_bytes=SMALL_BYTES),
        cost_estimate=pl.CostEstimate(
            flops=2 * rows * router.size, bytes_accessed=4 * router.size, transcendentals=0
        ),
    )(*[pltpu.with_memory_space_constraint(v, pltpu.HBM) for v in (tokens, expert_ids, router)])


def join_kernel(*refs):
    *parts, joined_ref = refs
    start = 0
    for part in parts:
        joined_ref[start : start + part.shape[0]] = part[...]
        start += part.shape[0]


def join(parts):
    rows, width = sum(part.shape[0] for part in parts), parts[0].shape[1]
    return pl.pallas_call(
        join_kernel,
        out_shape=pltpu.VMEM((rows, width), parts[0].dtype),
        in_specs=[IN_VMEM] * len(parts),
        out_specs=IN_VMEM,
        compiler_params=pltpu.CompilerParams(vmem_limit_bytes=SMALL_BYTES),
        cost_estimate=pl.CostEstimate(
            flops=EXCHANGE_FLOPS, bytes_accessed=0, transcendentals=0
        ),
    )(*parts)


def expert_kernel(exp_dev, expert_total, parts, *refs):
    pieces, refs = refs[:parts], refs[parts:]
    gate_ref, up_ref, down_ref, *results = refs
    units, width = down_ref.shape[1:]
    rows = jnp.concatenate([piece[...] for piece in pieces])
    tags = rows[:, width:].astype(jnp.float32)
    lane = lax.rem(lax.broadcasted_iota(jnp.int32, tags.shape, 1), expert_total)
    first_expert = lax.axis_index("dp") * exp_dev
    weights = [ref[local] for local in range(exp_dev) for ref in (gate_ref, up_ref)]
    both = times_rows(rows[:, :width], jnp.concatenate(weights))
    hidden, shares = [], []
    for local in range(exp_dev):
        middle = (2 * local + 1) * units
        gate, up = both[:, middle - units : middle], both[:, middle : middle + units]
        hidden.append((gate / (1.0 + jnp.exp(-gate)) * up).astype(jnp.bfloat16))
        mine = jnp.where(lane == first_expert + local, tags, 0.0)
        shares.append(jnp.sum(mine, axis=1, keepdims=True))
    block = min(2048, width)
    for first in range(0, width, block):
        total = 0.0
        for local in range(exp_dev):
            out = jnp.dot(
                hidden[local],
                down_ref[local, :, first : first + block],
                preferred_element_type=jnp.float32,
            )
            total = total + out * shares[local]
        start = 0
        for result in results:
            stop = start + result.shape[0]
            result[:, first : first + block] = total[start:stop].astype(result.dtype)
            start = stop


def run_experts(pieces, kinds, expert_total, w_gate, w_up, w_down):
    rows = sum(piece.shape[0] for piece in pieces)
    exp_dev, _, width = w_down.shape
    place = pltpu.VMEM if len(pieces) > 1 else jax.ShapeDtypeStruct
    return pl.pallas_call(
        functools.partial(expert_kernel, exp_dev, expert_total, len(pieces)),
        out_shape=[
            place((piece.shape[0], width), kind) for piece, kind in zip(pieces, kinds)
        ],
        in_specs=[IN_VMEM] * (len(pieces) + 3),
        out_specs=[IN_VMEM] * len(pieces),
        compiler_params=pltpu.CompilerParams(vmem_limit_bytes=VMEM_BYTES),
        cost_estimate=pl.CostEstimate(
            flops=6 * rows * w_down.size, bytes_accessed=rows * width * 5, transcendentals=0
        ),
    )(*pieces, w_gate, w_up, w_down)


def body(tokens, expert_ids, router, w_gate, w_up, w_down):
    pieces = gather_rows(pack(tokens, expert_ids, router))
    kinds = [jnp.float32] * 2 + [jnp.bfloat16] * 2
    operands = (router.shape[0], w_gate, w_up, w_down)
    if sum(piece.shape[0] for piece in pieces) <= ROWS:
        results = run_experts(pieces, kinds, *operands)
    else:
        results = []
        for piece, kind in zip(pieces, kinds):
            chunks = [
                run_experts([piece[start : start + ROWS]], [kind], *operands)[0]
                for start in range(0, piece.shape[0], ROWS)
            ]
            results.append(cat(chunks))
    return scatter_sums(results[:2], results[2:])


def solution(mesh):
    in_specs = (
        P(("dp", "expert"), None),
        P(("dp", "expert"), None),
        P(),
        P("dp", "expert", None),
        P("dp", "expert", None),
        P("dp", "expert", None),
    )
    out_specs = P(("dp", "expert"), None)
    return jax.shard_map(body, mesh=mesh, in_specs=in_specs, out_specs=out_specs, check_vma=False)
```

```python
import functools

import jax
import jax.numpy as jnp
from jax import lax
from jax.experimental import pallas as pl
from jax.experimental.pallas import tpu as pltpu
from jax.sharding import PartitionSpec as P

LANES = 128
ROWS = 256
TERMS = 3
VMEM_BYTES = 24 * 1024 * 1024
SMALL_BYTES = 2 * 1024 * 1024
EXCHANGE_FLOPS = 20_000_000_000
IN_VMEM = pl.BlockSpec(memory_space=pltpu.VMEM)
ANYWHERE = pl.BlockSpec(memory_space=pl.ANY)


def times_rows(left, right):
    return lax.dot_general(
        left, right, (((1,), (1,)), ((), ())), preferred_element_type=jnp.float32
    )


def swap(value, axis, mask):
    count = lax.axis_size(axis)
    return lax.ppermute(value, axis, [(i, i ^ mask) for i in range(count)])


def send(value, step):
    return swap(value.astype(jnp.bfloat16), *step)


def wide(value):
    return value.astype(jnp.float32)


CORE = ("dp", 1)


def plane_steps():
    return [("dp", mask) for mask in range(2, lax.axis_size("dp"), 2)]


def cat(parts):
    return parts[0] if len(parts) == 1 else jnp.concatenate(parts)


def split(value, count):
    step = value.shape[0] // count
    return [value[start : start + step] for start in range(0, value.shape[0], step)]


def after(value, *others):
    return lax.optimization_barrier((value, *others))[0]


def gather_rows(block):
    depth = lax.axis_size("expert")
    column = [block] + [swap(block, "expert", mask) for mask in range(1, depth)]
    near = join(column[: depth // 2])
    steps = plane_steps()
    near_rest = [swap(near, *step) for step in steps]
    far = cat(column[depth // 2 :])
    far_rest = [swap(far, *step) for step in steps]
    near = cat([near, *near_rest])
    near_there = swap(near, *CORE)
    far = cat([far, *far_rest])
    return [near, far, near_there, swap(far, *CORE)]


def kept_and_away(unit, count):
    sizes = [unit * (count + 1), unit * count, unit]
    return [(size, kind) for kind in (jnp.float32, jnp.bfloat16) for size in sizes]


def scatter_sums(*results):
    steps, depth = plane_steps(), lax.axis_size("expert")
    joined = [mine + wide(swap(other, *CORE)) for mine, other in zip(results[2::-1], results[:2:-1])]
    diagonal, (far, *rest), (near, *others) = [
        split(total, count) for total, count in zip(joined, (1, len(steps), len(steps) + 1))
    ]
    here = [send(other, step) for other, step in zip(diagonal + rest[::-1], steps[::-1])]
    others = [other.astype(jnp.bfloat16) for other in others[::-1]]
    here[0] = after(here[0], *others)
    others = [after(other, here[0]) for other in others]
    near_here = [send(other, step) for other, step in zip(others, steps[::-1])]
    sums = [sum([wide(other) for other in here], far), sum([wide(other) for other in near_here], near)]
    far, (total, *near) = split(sums[0], depth // 2), split(sums[1], depth // 2)
    far = [send(part, ("expert", mask + depth // 2)) for mask, part in enumerate(far)]
    near = [send(part, ("expert", mask + 1)) for mask, part in enumerate(near)]
    far = sum(wide(part) for part in far)
    far, *near = lax.optimization_barrier((far, *near))
    return sum([wide(part) for part in near], total + far).astype(jnp.bfloat16)


def pack_kernel(tokens_hbm, ids_hbm, router_hbm, packed_ref, tokens_ref, ids_ref, router_ref, done):
    pairs = [(tokens_hbm, tokens_ref), (ids_hbm, ids_ref), (router_hbm, router_ref)]
    copies = [
        pltpu.make_async_copy(source, target, done.at[index])
        for index, (source, target) in enumerate(pairs)
    ]
    for copy in copies:
        copy.start()
    for copy in copies:
        copy.wait()
    tokens = tokens_ref[...]
    width, expert_total = tokens.shape[1], router_ref.shape[0]
    logits = times_rows(tokens, router_ref[...])
    experts = lax.broadcasted_iota(jnp.int32, logits.shape, 1)
    ids = ids_ref[...]
    chosen = experts < 0
    for pick in range(ids.shape[1]):
        chosen = jnp.logical_or(chosen, ids[:, pick : pick + 1] == experts)
    scores = jnp.where(chosen, 1.0 / (1.0 + jnp.exp(-logits)), 0.0)
    rest = scores / jnp.sum(scores, axis=1, keepdims=True)
    place = (expert_total, packed_ref.shape[1] - width)
    source, lane = [lax.broadcasted_iota(jnp.int32, place, axis) for axis in (0, 1)]
    tags = 0.0
    for term in range(TERMS):
        part = rest.astype(jnp.bfloat16)
        rest = rest - part.astype(jnp.float32)
        moved = (lane == source + term * expert_total).astype(jnp.float32).astype(jnp.bfloat16)
        tags = tags + jnp.dot(part, moved, preferred_element_type=jnp.float32)
    packed_ref[:, :width] = tokens
    packed_ref[:, width:] = tags.astype(jnp.bfloat16)


def pack(tokens, expert_ids, router):
    rows, width = tokens.shape
    extra = -(-TERMS * router.shape[0] // LANES) * LANES
    return pl.pallas_call(
        pack_kernel,
        out_shape=pltpu.VMEM((rows, width + extra), tokens.dtype),
        in_specs=[ANYWHERE] * 3,
        out_specs=IN_VMEM,
        scratch_shapes=[
            *[pltpu.VMEM(value.shape, value.dtype) for value in (tokens, expert_ids, router)],
            pltpu.SemaphoreType.DMA((3,)),
        ],
        compiler_params=pltpu.CompilerParams(vmem_limit_bytes=SMALL_BYTES),
        cost_estimate=pl.CostEstimate(
            flops=2 * rows * router.size, bytes_accessed=4 * router.size, transcendentals=0
        ),
    )(*[pltpu.with_memory_space_constraint(v, pltpu.HBM) for v in (tokens, expert_ids, router)])


def join_kernel(*refs):
    *parts, joined_ref = refs
    start = 0
    for part in parts:
        joined_ref[start : start + part.shape[0]] = part[...]
        start += part.shape[0]


def join(parts):
    rows, width = sum(part.shape[0] for part in parts), parts[0].shape[1]
    return pl.pallas_call(
        join_kernel,
        out_shape=pltpu.VMEM((rows, width), parts[0].dtype),
        in_specs=[IN_VMEM] * len(parts),
        out_specs=IN_VMEM,
        compiler_params=pltpu.CompilerParams(vmem_limit_bytes=SMALL_BYTES),
        cost_estimate=pl.CostEstimate(
            flops=EXCHANGE_FLOPS, bytes_accessed=0, transcendentals=0
        ),
    )(*parts)


def expert_kernel(exp_dev, expert_total, parts, *refs):
    pieces, refs = refs[:parts], refs[parts:]
    gate_ref, up_ref, down_ref, *results = refs
    units, width = down_ref.shape[1:]
    rows = jnp.concatenate([piece[...] for piece in pieces])
    tags = rows[:, width:].astype(jnp.float32)
    lane = lax.rem(lax.broadcasted_iota(jnp.int32, tags.shape, 1), expert_total)
    first_expert = lax.axis_index("dp") * exp_dev
    weights = [ref[local] for local in range(exp_dev) for ref in (gate_ref, up_ref)]
    both = times_rows(rows[:, :width], jnp.concatenate(weights))
    hidden, shares = [], []
    for local in range(exp_dev):
        middle = (2 * local + 1) * units
        gate, up = both[:, middle - units : middle], both[:, middle : middle + units]
        hidden.append((gate / (1.0 + jnp.exp(-gate)) * up).astype(jnp.bfloat16))
        mine = jnp.where(lane == first_expert + local, tags, 0.0)
        shares.append(jnp.sum(mine, axis=1, keepdims=True))
    block = min(2048, width)
    for first in range(0, width, block):
        total = 0.0
        for local in range(exp_dev):
            out = jnp.dot(
                hidden[local],
                down_ref[local, :, first : first + block],
                preferred_element_type=jnp.float32,
            )
            total = total + out * shares[local]
        start = 0
        for result in results:
            stop = start + result.shape[0]
            result[:, first : first + block] = total[start:stop].astype(result.dtype)
            start = stop


def run_experts(pieces, results, expert_total, w_gate, w_up, w_down):
    rows = sum(piece.shape[0] for piece in pieces)
    exp_dev, _, width = w_down.shape
    place = pltpu.VMEM if len(results) > 1 else jax.ShapeDtypeStruct
    return pl.pallas_call(
        functools.partial(expert_kernel, exp_dev, expert_total, len(pieces)),
        out_shape=[place((size, width), kind) for size, kind in results],
        in_specs=[IN_VMEM] * (len(pieces) + 3),
        out_specs=[IN_VMEM] * len(results),
        compiler_params=pltpu.CompilerParams(vmem_limit_bytes=VMEM_BYTES),
        cost_estimate=pl.CostEstimate(
            flops=6 * rows * w_down.size, bytes_accessed=rows * width * 5, transcendentals=0
        ),
    )(*pieces, w_gate, w_up, w_down)


def body(tokens, expert_ids, router, w_gate, w_up, w_down):
    pieces = gather_rows(pack(tokens, expert_ids, router))
    count = len(plane_steps())
    results = kept_and_away(pieces[0].shape[0] // (count + 1), count)
    operands = (router.shape[0], w_gate, w_up, w_down)
    rows = sum(piece.shape[0] for piece in pieces)
    if rows <= ROWS:
        return scatter_sums(*run_experts(pieces, results, *operands))
    pieces = cat(pieces)
    outputs = cat([
        run_experts([pieces[first : first + ROWS]], [(ROWS, jnp.float32)], *operands)[0]
        for first in range(0, rows, ROWS)
    ])
    parts, start = [], 0
    for size, kind in results:
        parts.append(outputs[start : start + size].astype(kind))
        start += size
    return scatter_sums(*parts)


def solution(mesh):
    in_specs = (
        P(("dp", "expert"), None),
        P(("dp", "expert"), None),
        P(),
        P("dp", "expert", None),
        P("dp", "expert", None),
        P("dp", "expert", None),
    )
    out_specs = P(("dp", "expert"), None)
    return jax.shard_map(body, mesh=mesh, in_specs=in_specs, out_specs=out_specs, check_vma=False)
```

```python
import functools

import jax
import jax.numpy as jnp
from jax import lax
from jax.experimental import pallas as pl
from jax.experimental.pallas import tpu as pltpu
from jax.sharding import PartitionSpec as P

LANES = 128
ROWS = 256
TERMS = 3
VMEM_BYTES = 24 * 1024 * 1024
SMALL_BYTES = 2 * 1024 * 1024
EXCHANGE_FLOPS = 20_000_000_000
IN_VMEM = pl.BlockSpec(memory_space=pltpu.VMEM)
ANYWHERE = pl.BlockSpec(memory_space=pl.ANY)


def times_rows(left, right):
    return lax.dot_general(
        left, right, (((1,), (1,)), ((), ())), preferred_element_type=jnp.float32
    )


def swap(value, axis, mask):
    count = lax.axis_size(axis)
    return lax.ppermute(value, axis, [(i, i ^ mask) for i in range(count)])


def send(value, step):
    return swap(value.astype(jnp.bfloat16), *step)


def wide(value):
    return value.astype(jnp.float32)


CORE = ("dp", 1)


def plane_steps():
    return [("dp", mask) for mask in range(2, lax.axis_size("dp"), 2)]


def cat(parts):
    return parts[0] if len(parts) == 1 else jnp.concatenate(parts)


def split(value, count):
    step = value.shape[0] // count
    return [value[start : start + step] for start in range(0, value.shape[0], step)]


def after(value, *others):
    return lax.optimization_barrier((value, *others))[0]


def gather_rows(block):
    depth = lax.axis_size("expert")
    column = [block] + [swap(block, "expert", mask) for mask in range(1, depth)]
    near = join(column[: depth // 2])
    steps = plane_steps()
    near_rest = [swap(near, *step) for step in steps]
    far = cat(column[depth // 2 :])
    far_rest = [swap(far, *step) for step in steps]
    near = cat([near, *near_rest])
    near_there = swap(near, *CORE)
    far = cat([far, *far_rest])
    return [near, far, near_there, swap(far, *CORE)]


def kept_and_away(unit, count):
    sizes = [unit * (count + 1), unit * count, unit]
    return [(size, kind) for kind in (jnp.float32, jnp.bfloat16) for size in sizes]


def scatter_sums(*results):
    steps, depth = plane_steps(), lax.axis_size("expert")
    joined = [mine + wide(swap(other, *CORE)) for mine, other in zip(results[2::-1], results[:2:-1])]
    diagonal, (far, *rest), (near, *others) = [
        split(total, count) for total, count in zip(joined, (1, len(steps), len(steps) + 1))
    ]
    here = [send(other, step) for other, step in zip(diagonal + rest[::-1], steps[::-1])]
    others = [other.astype(jnp.bfloat16) for other in others[::-1]]
    here[0] = after(here[0], *others)
    others = [after(other, here[0]) for other in others]
    near_here = [send(other, step) for other, step in zip(others, steps[::-1])]
    sums = [sum([wide(other) for other in here], far), sum([wide(other) for other in near_here], near)]
    far, (total, *near) = split(sums[0], depth // 2), split(sums[1], depth // 2)
    far = [send(part, ("expert", mask + depth // 2)) for mask, part in enumerate(far)]
    near = [send(part, ("expert", mask + 1)) for mask, part in enumerate(near)]
    far = sum(wide(part) for part in far)
    far, *near = lax.optimization_barrier((far, *near))
    return sum([wide(part) for part in near], total + far).astype(jnp.bfloat16)


def pack_kernel(tokens_hbm, ids_hbm, router_hbm, packed_ref, tokens_ref, ids_ref, router_ref, done):
    pairs = [(tokens_hbm, tokens_ref), (ids_hbm, ids_ref), (router_hbm, router_ref)]
    copies = [
        pltpu.make_async_copy(source, target, done.at[index])
        for index, (source, target) in enumerate(pairs)
    ]
    for copy in copies:
        copy.start()
    for copy in copies:
        copy.wait()
    tokens = tokens_ref[...]
    width, expert_total = tokens.shape[1], router_ref.shape[0]
    logits = times_rows(tokens, router_ref[...])
    experts = lax.broadcasted_iota(jnp.int32, logits.shape, 1)
    ids = ids_ref[...]
    chosen = experts < 0
    for pick in range(ids.shape[1]):
        chosen = jnp.logical_or(chosen, ids[:, pick : pick + 1] == experts)
    scores = jnp.where(chosen, 1.0 / (1.0 + jnp.exp(-logits)), 0.0)
    rest = scores / jnp.sum(scores, axis=1, keepdims=True)
    place = (expert_total, packed_ref.shape[1] - width)
    source, lane = [lax.broadcasted_iota(jnp.int32, place, axis) for axis in (0, 1)]
    tags = 0.0
    for term in range(TERMS):
        part = rest.astype(jnp.bfloat16)
        rest = rest - part.astype(jnp.float32)
        moved = (lane == source + term * expert_total).astype(jnp.float32).astype(jnp.bfloat16)
        tags = tags + jnp.dot(part, moved, preferred_element_type=jnp.float32)
    packed_ref[:, :width] = tokens
    packed_ref[:, width:] = tags.astype(jnp.bfloat16)


def pack(tokens, expert_ids, router):
    rows, width = tokens.shape
    extra = -(-TERMS * router.shape[0] // LANES) * LANES
    return pl.pallas_call(
        pack_kernel,
        out_shape=pltpu.VMEM((rows, width + extra), tokens.dtype),
        in_specs=[ANYWHERE] * 3,
        out_specs=IN_VMEM,
        scratch_shapes=[
            *[pltpu.VMEM(value.shape, value.dtype) for value in (tokens, expert_ids, router)],
            pltpu.SemaphoreType.DMA((3,)),
        ],
        compiler_params=pltpu.CompilerParams(vmem_limit_bytes=SMALL_BYTES),
        cost_estimate=pl.CostEstimate(
            flops=2 * rows * router.size, bytes_accessed=4 * router.size, transcendentals=0
        ),
    )(*[pltpu.with_memory_space_constraint(v, pltpu.HBM) for v in (tokens, expert_ids, router)])


def join_kernel(*refs):
    *parts, joined_ref = refs
    start = 0
    for part in parts:
        joined_ref[start : start + part.shape[0]] = part[...]
        start += part.shape[0]


def join(parts):
    rows, width = sum(part.shape[0] for part in parts), parts[0].shape[1]
    return pl.pallas_call(
        join_kernel,
        out_shape=pltpu.VMEM((rows, width), parts[0].dtype),
        in_specs=[IN_VMEM] * len(parts),
        out_specs=IN_VMEM,
        compiler_params=pltpu.CompilerParams(vmem_limit_bytes=SMALL_BYTES),
        cost_estimate=pl.CostEstimate(
            flops=EXCHANGE_FLOPS, bytes_accessed=0, transcendentals=0
        ),
    )(*parts)


def expert_kernel(exp_dev, expert_total, parts, *refs):
    pieces, refs = refs[:parts], refs[parts:]
    gate_ref, up_ref, down_ref, *results = refs
    units, width = down_ref.shape[1:]
    rows = jnp.concatenate([piece[...] for piece in pieces])
    tags = rows[:, width:].astype(jnp.float32)
    lane = lax.rem(lax.broadcasted_iota(jnp.int32, tags.shape, 1), expert_total)
    first_expert = lax.axis_index("dp") * exp_dev
    weights = [ref[local] for local in range(exp_dev) for ref in (gate_ref, up_ref)]
    both = times_rows(rows[:, :width], jnp.concatenate(weights))
    hidden = []
    for local in range(exp_dev):
        middle = (2 * local + 1) * units
        gate, up = both[:, middle - units : middle], both[:, middle : middle + units]
        mine = jnp.where(lane == first_expert + local, tags, 0.0)
        share = jnp.sum(mine, axis=1, keepdims=True)
        hidden.append((gate / (1.0 + jnp.exp(-gate)) * up * share).astype(jnp.bfloat16))
    hidden = jnp.concatenate(hidden, axis=1)
    block = min(2048, width)
    for first in range(0, width, block):
        down = down_ref[:, :, first : first + block].reshape(exp_dev * units, block)
        total = jnp.dot(hidden, down, preferred_element_type=jnp.float32)
        start = 0
        for result in results:
            stop = start + result.shape[0]
            result[:, first : first + block] = total[start:stop].astype(result.dtype)
            start = stop


def run_experts(pieces, results, expert_total, w_gate, w_up, w_down):
    rows = sum(piece.shape[0] for piece in pieces)
    exp_dev, _, width = w_down.shape
    place = pltpu.VMEM if len(results) > 1 else jax.ShapeDtypeStruct
    return pl.pallas_call(
        functools.partial(expert_kernel, exp_dev, expert_total, len(pieces)),
        out_shape=[place((size, width), kind) for size, kind in results],
        in_specs=[IN_VMEM] * (len(pieces) + 3),
        out_specs=[IN_VMEM] * len(results),
        compiler_params=pltpu.CompilerParams(vmem_limit_bytes=VMEM_BYTES),
        cost_estimate=pl.CostEstimate(
            flops=6 * rows * w_down.size, bytes_accessed=rows * width * 5, transcendentals=0
        ),
    )(*pieces, w_gate, w_up, w_down)


def body(tokens, expert_ids, router, w_gate, w_up, w_down):
    pieces = gather_rows(pack(tokens, expert_ids, router))
    count = len(plane_steps())
    results = kept_and_away(pieces[0].shape[0] // (count + 1), count)
    operands = (router.shape[0], w_gate, w_up, w_down)
    rows = sum(piece.shape[0] for piece in pieces)
    if rows <= ROWS:
        return scatter_sums(*run_experts(pieces, results, *operands))
    pieces = cat(pieces)
    outputs = cat([
        run_experts([pieces[first : first + ROWS]], [(ROWS, jnp.float32)], *operands)[0]
        for first in range(0, rows, ROWS)
    ])
    parts, start = [], 0
    for size, kind in results:
        parts.append(outputs[start : start + size].astype(kind))
        start += size
    return scatter_sums(*parts)


def solution(mesh):
    in_specs = (
        P(("dp", "expert"), None),
        P(("dp", "expert"), None),
        P(),
        P("dp", "expert", None),
        P("dp", "expert", None),
        P("dp", "expert", None),
    )
    out_specs = P(("dp", "expert"), None)
    return jax.shard_map(body, mesh=mesh, in_specs=in_specs, out_specs=out_specs, check_vma=False)
```

```python
import functools

import jax
import jax.numpy as jnp
from jax import lax
from jax.experimental import pallas as pl
from jax.experimental.pallas import tpu as pltpu
from jax.sharding import PartitionSpec as P

LANES = 128
ROWS = 256
TERMS = 3
VMEM_BYTES = 24 * 1024 * 1024
SMALL_BYTES = 2 * 1024 * 1024
EXCHANGE_FLOPS = 20_000_000_000
IN_VMEM = pl.BlockSpec(memory_space=pltpu.VMEM)
ANYWHERE = pl.BlockSpec(memory_space=pl.ANY)


def times_rows(left, right):
    return lax.dot_general(
        left, right, (((1,), (1,)), ((), ())), preferred_element_type=jnp.float32
    )


def swap(value, axis, mask):
    count = lax.axis_size(axis)
    return lax.ppermute(value, axis, [(i, i ^ mask) for i in range(count)])


def send(value, step):
    return swap(value.astype(jnp.bfloat16), *step)


def wide(value):
    return value.astype(jnp.float32)


CORE = ("dp", 1)


def plane_steps():
    return [("dp", mask) for mask in range(2, lax.axis_size("dp"), 2)]


def cat(parts):
    return parts[0] if len(parts) == 1 else jnp.concatenate(parts)


def split(value, count):
    step = value.shape[0] // count
    return [value[start : start + step] for start in range(0, value.shape[0], step)]


def after(value, *others):
    return lax.optimization_barrier((value, *others))[0]


def gather_rows(block):
    depth = lax.axis_size("expert")
    column = [block] + [swap(block, "expert", mask) for mask in range(1, depth)]
    near = join(column[: depth // 2])
    steps = plane_steps()
    near_rest = [swap(near, *step) for step in steps]
    far = cat(column[depth // 2 :])
    far_rest = [swap(far, *step) for step in steps]
    near = cat([near, *near_rest])
    near_there = swap(near, *CORE)
    far = cat([far, *far_rest])
    return [near, far, near_there, swap(far, *CORE)]


def kept_and_away(unit, count):
    sizes = [unit * (count + 1), unit * count, unit]
    return [(size, kind) for kind in (jnp.float32, jnp.bfloat16) for size in sizes]


def scatter_sums(*results):
    steps, depth = plane_steps(), lax.axis_size("expert")
    joined = [mine + wide(swap(other, *CORE)) for mine, other in zip(results[2::-1], results[:2:-1])]
    diagonal, (far, *rest), (near, *others) = [
        split(total, count) for total, count in zip(joined, (1, len(steps), len(steps) + 1))
    ]
    here = [send(other, step) for other, step in zip(diagonal + rest[::-1], steps[::-1])]
    others = [other.astype(jnp.bfloat16) for other in others[::-1]]
    here[0] = after(here[0], *others)
    others = [after(other, here[0]) for other in others]
    near_here = [send(other, step) for other, step in zip(others, steps[::-1])]
    sums = [sum([wide(other) for other in here], far), sum([wide(other) for other in near_here], near)]
    far, (total, *near) = split(sums[0], depth // 2), split(sums[1], depth // 2)
    far = [send(part, ("expert", mask + depth // 2)) for mask, part in enumerate(far)][::-1]
    near = [send(part, ("expert", mask + 1)) for mask, part in enumerate(near)]
    far = sum(wide(part) for part in far)
    far, *near = lax.optimization_barrier((far, *near))
    return sum([wide(part) for part in near], total + far).astype(jnp.bfloat16)


def pack_kernel(tokens_hbm, ids_hbm, router_hbm, packed_ref, tokens_ref, ids_ref, router_ref, done):
    pairs = [(tokens_hbm, tokens_ref), (ids_hbm, ids_ref), (router_hbm, router_ref)]
    copies = [
        pltpu.make_async_copy(source, target, done.at[index])
        for index, (source, target) in enumerate(pairs)
    ]
    for copy in copies:
        copy.start()
    for copy in copies:
        copy.wait()
    tokens = tokens_ref[...]
    width, expert_total = tokens.shape[1], router_ref.shape[0]
    logits = times_rows(tokens, router_ref[...])
    experts = lax.broadcasted_iota(jnp.int32, logits.shape, 1)
    ids = ids_ref[...]
    chosen = experts < 0
    for pick in range(ids.shape[1]):
        chosen = jnp.logical_or(chosen, ids[:, pick : pick + 1] == experts)
    scores = jnp.where(chosen, 1.0 / (1.0 + jnp.exp(-logits)), 0.0)
    rest = scores / jnp.sum(scores, axis=1, keepdims=True)
    place = (expert_total, packed_ref.shape[1] - width)
    source, lane = [lax.broadcasted_iota(jnp.int32, place, axis) for axis in (0, 1)]
    tags = 0.0
    for term in range(TERMS):
        part = rest.astype(jnp.bfloat16)
        rest = rest - part.astype(jnp.float32)
        moved = (lane == source + term * expert_total).astype(jnp.float32).astype(jnp.bfloat16)
        tags = tags + jnp.dot(part, moved, preferred_element_type=jnp.float32)
    packed_ref[:, :width] = tokens
    packed_ref[:, width:] = tags.astype(jnp.bfloat16)


def pack(tokens, expert_ids, router):
    rows, width = tokens.shape
    extra = -(-TERMS * router.shape[0] // LANES) * LANES
    return pl.pallas_call(
        pack_kernel,
        out_shape=pltpu.VMEM((rows, width + extra), tokens.dtype),
        in_specs=[ANYWHERE] * 3,
        out_specs=IN_VMEM,
        scratch_shapes=[
            *[pltpu.VMEM(value.shape, value.dtype) for value in (tokens, expert_ids, router)],
            pltpu.SemaphoreType.DMA((3,)),
        ],
        compiler_params=pltpu.CompilerParams(vmem_limit_bytes=SMALL_BYTES),
        cost_estimate=pl.CostEstimate(
            flops=2 * rows * router.size, bytes_accessed=4 * router.size, transcendentals=0
        ),
    )(*[pltpu.with_memory_space_constraint(v, pltpu.HBM) for v in (tokens, expert_ids, router)])


def join_kernel(*refs):
    *parts, joined_ref = refs
    start = 0
    for part in parts:
        joined_ref[start : start + part.shape[0]] = part[...]
        start += part.shape[0]


def join(parts):
    rows, width = sum(part.shape[0] for part in parts), parts[0].shape[1]
    return pl.pallas_call(
        join_kernel,
        out_shape=pltpu.VMEM((rows, width), parts[0].dtype),
        in_specs=[IN_VMEM] * len(parts),
        out_specs=IN_VMEM,
        compiler_params=pltpu.CompilerParams(vmem_limit_bytes=SMALL_BYTES),
        cost_estimate=pl.CostEstimate(
            flops=EXCHANGE_FLOPS, bytes_accessed=0, transcendentals=0
        ),
    )(*parts)


def expert_kernel(exp_dev, expert_total, parts, *refs):
    pieces, refs = refs[:parts], refs[parts:]
    gate_ref, up_ref, down_ref, *results = refs
    units, width = down_ref.shape[1:]
    rows = jnp.concatenate([piece[...] for piece in pieces])
    tags = rows[:, width:].astype(jnp.float32)
    lane = lax.rem(lax.broadcasted_iota(jnp.int32, tags.shape, 1), expert_total)
    first_expert = lax.axis_index("dp") * exp_dev
    weights = [ref[local] for local in range(exp_dev) for ref in (gate_ref, up_ref)]
    both = times_rows(rows[:, :width], jnp.concatenate(weights))
    hidden = []
    for local in range(exp_dev):
        middle = (2 * local + 1) * units
        gate, up = both[:, middle - units : middle], both[:, middle : middle + units]
        mine = jnp.where(lane == first_expert + local, tags, 0.0)
        share = jnp.sum(mine, axis=1, keepdims=True)
        hidden.append((gate / (1.0 + jnp.exp(-gate)) * up * share).astype(jnp.bfloat16))
    hidden = jnp.concatenate(hidden, axis=1)
    block = min(2048, width)
    for first in range(0, width, block):
        down = down_ref[:, :, first : first + block].reshape(exp_dev * units, block)
        total = jnp.dot(hidden, down, preferred_element_type=jnp.float32)
        start = 0
        for result in results:
            stop = start + result.shape[0]
            result[:, first : first + block] = total[start:stop].astype(result.dtype)
            start = stop


def run_experts(pieces, results, expert_total, w_gate, w_up, w_down):
    rows = sum(piece.shape[0] for piece in pieces)
    exp_dev, _, width = w_down.shape
    place = pltpu.VMEM if len(results) > 1 else jax.ShapeDtypeStruct
    return pl.pallas_call(
        functools.partial(expert_kernel, exp_dev, expert_total, len(pieces)),
        out_shape=[place((size, width), kind) for size, kind in results],
        in_specs=[IN_VMEM] * (len(pieces) + 3),
        out_specs=[IN_VMEM] * len(results),
        compiler_params=pltpu.CompilerParams(vmem_limit_bytes=VMEM_BYTES),
        cost_estimate=pl.CostEstimate(
            flops=6 * rows * w_down.size, bytes_accessed=rows * width * 5, transcendentals=0
        ),
    )(*pieces, w_gate, w_up, w_down)


def body(tokens, expert_ids, router, w_gate, w_up, w_down):
    pieces = gather_rows(pack(tokens, expert_ids, router))
    count = len(plane_steps())
    results = kept_and_away(pieces[0].shape[0] // (count + 1), count)
    operands = (router.shape[0], w_gate, w_up, w_down)
    rows = sum(piece.shape[0] for piece in pieces)
    if rows <= ROWS:
        return scatter_sums(*run_experts(pieces, results, *operands))
    pieces = cat(pieces)
    outputs = cat([
        run_experts([pieces[first : first + ROWS]], [(ROWS, jnp.float32)], *operands)[0]
        for first in range(0, rows, ROWS)
    ])
    parts, start = [], 0
    for size, kind in results:
        parts.append(outputs[start : start + size].astype(kind))
        start += size
    return scatter_sums(*parts)


def solution(mesh):
    in_specs = (
        P(("dp", "expert"), None),
        P(("dp", "expert"), None),
        P(),
        P("dp", "expert", None),
        P("dp", "expert", None),
        P("dp", "expert", None),
    )
    out_specs = P(("dp", "expert"), None)
    return jax.shard_map(body, mesh=mesh, in_specs=in_specs, out_specs=out_specs, check_vma=False)
```
